128 devices in a mesh: section: 2 (over core), row: 4 (over y), col: 16 (over x, z).
Axes of the slice: x: 4, y: 4, z: 4, core: 2. Of those that a mesh axis runs over, the one named last changes fastest.
Arguments:
- block_input: bfloat16 [2, 4096, 1024], P(None, 'col', 'row'), may hold values from -30 to 30
- cotangent: bfloat16 [2, 4096, 1024], P(None, 'col', 'row'), may hold values from -6 to 6
- images_used: int32 [2], replicated, may hold values from 1 to 4, as said below
- norm1_gain: float32 [2, 1024], P('section', 'row'), may hold values from 0.5 to 1.5
- norm1_bias: float32 [2, 1024], P('section', 'row'), may hold values from -1.75 to 1.75
- qkv_weight: bfloat16 [2, 1024, 3072], P('section', 'row', 'col'), may hold values from -0.1875 to 0.1875
- query_bias: float32 [2, 1024], P('section', 'col'), may hold values from -1.75 to 1.75
- value_bias: float32 [2, 1024], P('section', 'col'), may hold values from -0.625 to 0.625
- proj_weight: bfloat16 [2, 1024, 1024], P('section', 'col', 'row'), may hold values from -1.5 to 1.5
- proj_bias: float32 [2, 1024], P('section', 'row'), may hold values from -1.75 to 1.75
- attn_scale: float32 [2, 1024], P('section', 'row'), may hold values from 0.5 to 1.5
- norm2_gain: float32 [2, 1024], P('section', 'row'), may hold values from 0.5 to 1.5
- norm2_bias: float32 [2, 1024], P('section', 'row'), may hold values from -1.75 to 1.75
- inner_weight: bfloat16 [2, 1024, 4096], P('section', 'row', 'col'), may hold values from -0.1875 to 0.1875
- inner_bias: float32 [2, 4096], P('section', 'col'), may hold values from -1.75 to 1.75
- outer_weight: bfloat16 [2, 4096, 1024], P('section', 'col', 'row'), may hold values from -0.09375 to 0.09375
- outer_bias: float32 [2, 1024], P('section', 'row'), may hold values from -1.75 to 1.75
- mlp_scale: float32 [2, 1024], P('section', 'row'), may hold values from 0.5 to 1.5
Outputs:
- boundary: float32 [2, 2, 4096, 1024], P('section', None, 'col', 'row')
- grad_norm1_gain: float32 [2, 1024], P('section', 'row')
- grad_norm1_bias: float32 [2, 1024], P('section', 'row')
- grad_qkv_weight: float32 [2, 1024, 3072], P('section', 'row', 'col')
- grad_query_bias: float32 [2, 1024], P('section', 'col')
- grad_value_bias: float32 [2, 1024], P('section', 'col')
- grad_proj_weight: float32 [2, 1024, 1024], P('section', 'col', 'row')
- grad_proj_bias: float32 [2, 1024], P('section', 'row')
- grad_attn_scale: float32 [2, 1024], P('section', 'row')
- grad_norm2_gain: float32 [2, 1024], P('section', 'row')
- grad_norm2_bias: float32 [2, 1024], P('section', 'row')
- grad_inner_weight: float32 [2, 1024, 4096], P('section', 'row', 'col')
- grad_inner_bias: float32 [2, 4096], P('section', 'col')
- grad_outer_weight: float32 [2, 4096, 1024], P('section', 'col', 'row')
- grad_outer_bias: float32 [2, 1024], P('section', 'row')
- grad_mlp_scale: float32 [2, 1024], P('section', 'row')
The draws below stay inside these ranges and needn't reach their ends.
Inputs may be any that keep to these rules, and one draw needn't show every extreme that they name: Micro-batch m holds images in its first images_used[m] slots of 1024 tokens; its other slots are empty. Some micro-batch is full in every draw.
All inputs are finite; a program needn't handle non-finite values.
Results may differ from the reference program's by a relative error of at most 0.02.
Values may be sent and summed in bfloat16 or wider, within the bound.
No kernel may reach another device: no remote copies, remote signals or barrier semaphores. Data moves between devices by JAX's collectives and lax.ppermute only.
A program may use at most 192 MiB of HBM per device.

```python
import jax
import jax.numpy as jnp
from jax import lax

D = 1024
HEADS = 16
HD = 64
FF = 4096
LENGTH = 1024
NMB = 2
SLOTS = 4
MB_TOK = 4096
N_SECTION = 2


def draw_block_input(key, part):
    key = jax.random.fold_in(key, 11)
    base_key, column_key, row_key = jax.random.split(key, 3)
    position = jnp.arange(D, dtype=jnp.float32) / max(D - 1, 1)
    columns = jnp.exp(position * 1.0986123) * jnp.exp(jax.random.uniform(column_key, (D,), jnp.float32, 0.0, 1.2)) / 3.0
    rows = jnp.exp(jax.random.uniform(row_key, (NMB, SLOTS * LENGTH, 1), jnp.float32, -0.5, 0.5))
    base = jnp.clip(jax.random.normal(base_key, (NMB, SLOTS * LENGTH, D), jnp.float32), -5.0, 5.0)
    return (base * columns * rows).astype(jnp.bfloat16)


def draw_images_used(key, part):
    key = jax.random.fold_in(key, 23)
    full_key, count_key = jax.random.split(key, 2)
    full_batch = jax.random.randint(full_key, (), 0, NMB, dtype=jnp.int32)
    counts = jax.random.randint(count_key, (NMB,), 1, SLOTS, dtype=jnp.int32)
    batch_ids = jnp.arange(NMB, dtype=jnp.int32)
    return jnp.where(batch_ids == full_batch, jnp.int32(SLOTS), counts).astype(jnp.int32)


def block_levels(stream_key, shape, shards, low, top_value):
    def one(dim, shards_of):
        draws = jax.random.uniform(jax.random.fold_in(jax.random.fold_in(stream_key, 6), dim), (shards_of,), jnp.float32, low / len(shards), top_value / len(shards))
        return jnp.repeat(jnp.exp(draws), shape[dim] // shards_of).reshape((-1,) + (1,) * (len(shape) - dim - 1))

    loudness = one(*shards[0])
    for cut in shards[1:]:
        loudness = loudness * one(*cut)
    return loudness


def bell_draw(key, shape, scale, bound, pieces=(), kind=jnp.bfloat16):
    array = scale * jax.random.normal(key, shape, jnp.float32)
    if pieces:
        array = array * block_levels(key, shape, pieces, -0.22, 0.18)
    return jnp.clip(array, -bound, bound).astype(kind)


def setup_inputs(seed: int = 0) -> dict:
    key_list = jax.random.split(jax.random.key(seed), 19)
    block_input = draw_block_input(jax.random.fold_in(key_list[18], 71), 0)
    cotangent = bell_draw(key_list[1], (NMB, MB_TOK, D), 1.0, 6.0, ((1, 16), (2, 4)))
    images_used = draw_images_used(jax.random.fold_in(key_list[18], 71), 0)
    norm1_gain = jnp.clip(1.0 + 0.1 * jax.random.normal(key_list[3], (N_SECTION, D), jnp.float32), 0.5, 1.5)
    norm1_bias = bell_draw(key_list[4], (N_SECTION, D), 0.3, 1.75, ((0, 2), (1, 4)), jnp.float32)
    qkv_weight = bell_draw(key_list[5], (N_SECTION, D, 3 * D), D ** -0.5, 0.1875, ((0, 2), (1, 4), (2, 16)))
    query_bias = bell_draw(key_list[6], (N_SECTION, D), 0.3, 1.75, ((0, 2), (1, 16)), jnp.float32)
    value_bias = bell_draw(key_list[7], (N_SECTION, D), 0.1, 0.625, ((0, 2), (1, 16)), jnp.float32)
    proj_weight = bell_draw(key_list[8], (N_SECTION, D, D), (D // 64) ** -0.5, 1.5, ((0, 2), (1, 16), (2, 4)))
    proj_bias = bell_draw(key_list[9], (N_SECTION, D), 0.3, 1.75, ((0, 2), (1, 4)), jnp.float32)
    attn_scale = jnp.clip(1.0 + 0.1 * jax.random.normal(key_list[10], (N_SECTION, D), jnp.float32), 0.5, 1.5)
    norm2_gain = jnp.clip(1.0 + 0.1 * jax.random.normal(key_list[11], (N_SECTION, D), jnp.float32), 0.5, 1.5)
    norm2_bias = bell_draw(key_list[12], (N_SECTION, D), 0.3, 1.75, ((0, 2), (1, 4)), jnp.float32)
    inner_weight = bell_draw(key_list[13], (N_SECTION, D, FF), D ** -0.5, 0.1875, ((0, 2), (1, 4), (2, 16)))
    inner_bias = bell_draw(key_list[14], (N_SECTION, FF), 0.3, 1.75, ((0, 2), (1, 16)), jnp.float32)
    outer_weight = bell_draw(key_list[15], (N_SECTION, FF, D), FF ** -0.5, 0.09375, ((0, 2), (1, 16), (2, 4)))
    outer_bias = bell_draw(key_list[16], (N_SECTION, D), 0.3, 1.75, ((0, 2), (1, 4)), jnp.float32)
    mlp_scale = jnp.clip(1.0 + 0.1 * jax.random.normal(key_list[17], (N_SECTION, D), jnp.float32), 0.5, 1.5)
    return {"block_input": block_input, "cotangent": cotangent, "images_used": images_used, "norm1_gain": norm1_gain, "norm1_bias": norm1_bias, "qkv_weight": qkv_weight, "query_bias": query_bias, "value_bias": value_bias, "proj_weight": proj_weight, "proj_bias": proj_bias, "attn_scale": attn_scale, "norm2_gain": norm2_gain, "norm2_bias": norm2_bias, "inner_weight": inner_weight, "inner_bias": inner_bias, "outer_weight": outer_weight, "outer_bias": outer_bias, "mlp_scale": mlp_scale}


@jax.custom_vjp
def low(v):
    return lax.optimization_barrier(v.astype(jnp.bfloat16)).astype(jnp.float32)

@jax.custom_vjp
def low_back(v):
    return v

def low_keep(v):
    return (low(v), None)

def low_pass(kept, grad):
    return (grad,)

def back_keep(v):
    return (v, None)

def back_low(kept, grad):
    return (low(grad),)
low.defvjp(low_keep, low_pass)
low_back.defvjp(back_keep, back_low)
norm_eps = 1e-06

def matmul(left_side, right_side):
    return jnp.dot(left_side, right_side, precision=lax.Precision.HIGHEST, preferred_element_type=jnp.float32)

def layer_norm(features, norm_gain, norm_shift):
    center = lax.optimization_barrier(jnp.mean(features, axis=-1, keepdims=True))
    offset = features - center
    spread = lax.optimization_barrier(jnp.mean(offset * offset, axis=-1, keepdims=True))
    return offset * lax.rsqrt(spread + norm_eps) * norm_gain + norm_shift

def image_attention(triples):
    queries = triples[:, :, 0, :]
    key_rows = triples[:, :, 1, :]
    values = triples[:, :, 2, :]
    scores = low_back(jnp.einsum('qhd,khd->hqk', queries, key_rows, precision=lax.Precision.HIGHEST) * HD ** (-0.5))
    attn_probs = jax.nn.softmax(scores, axis=-1)
    mixed_heads = jnp.einsum('hqk,khd->qhd', low(attn_probs), values, precision=lax.Precision.HIGHEST)
    return low(low_back(mixed_heads.reshape(LENGTH, HEADS * HD)))

def encoder_block(features, layer_params):
    gain_one, shift_one, joint_weight, query_bias, value_bias, proj_weight, proj_bias, scale_one, gain_two, shift_two, inner_weight, inner_bias, outer_weight, outer_bias, scale_two = layer_params
    normed = low(layer_norm(features, gain_one, shift_one))
    joint_bias = jnp.stack([query_bias.reshape(HEADS, HD), jnp.zeros((HEADS, HD), query_bias.dtype), value_bias.reshape(HEADS, HD)], axis=1).reshape(3 * D)
    triples = low(low_back(matmul(normed, joint_weight) + joint_bias))
    images = triples.reshape(SLOTS, LENGTH, HEADS, 3, HD)
    heads_out = lax.map(jax.checkpoint(image_attention), images).reshape(SLOTS * LENGTH, D)
    attended = low_back(matmul(heads_out, proj_weight) + proj_bias)
    hidden = features + scale_one * attended
    second = low(layer_norm(hidden, gain_two, shift_two))
    expanded = low_back(matmul(second, inner_weight) + inner_bias)
    active = low(jax.nn.gelu(expanded, approximate=False))
    contracted = low_back(matmul(active, outer_weight) + outer_bias)
    return hidden + scale_two * contracted

def section_forward(section_params, features, live_mask):
    first_params = tuple((stacked[0] for stacked in section_params))
    second_params = tuple((stacked[1] for stacked in section_params))
    handed = low(low_back(encoder_block(features, first_params)))
    return encoder_block(handed, second_params) * live_mask

def reference(block_input, cotangent, images_used, norm1_gain, norm1_bias, qkv_weight, query_bias, value_bias, proj_weight, proj_bias, attn_scale, norm2_gain, norm2_bias, inner_weight, inner_bias, outer_weight, outer_bias, mlp_scale):
    params = tuple((stacked.astype(jnp.float32) for stacked in (norm1_gain, norm1_bias, qkv_weight, query_bias, value_bias, proj_weight, proj_bias, attn_scale, norm2_gain, norm2_bias, inner_weight, inner_bias, outer_weight, outer_bias, mlp_scale)))

    def batch_step(totals, batch_items):
        tokens_in, cot_rows, used_count = batch_items
        slot_of = jnp.arange(SLOTS * LENGTH, dtype=jnp.int32) // LENGTH
        live_mask = (slot_of < used_count).astype(jnp.float32)[:, None]

        def masked(all_params, features):
            return section_forward(all_params, features, live_mask)
        result, pullback = jax.vjp(masked, params, tokens_in.astype(jnp.float32))
        param_grads, input_grad = pullback(cot_rows.astype(jnp.float32))
        return (jax.tree.map(jnp.add, totals, param_grads), (input_grad, result))
    start_totals = jax.tree.map(jnp.zeros_like, params)
    totals, (input_grads, outputs) = lax.scan(batch_step, start_totals, (block_input, cotangent, images_used))
    boundary = jnp.stack([input_grads, outputs], axis=0)
    return (boundary, totals[0], totals[1], totals[2], totals[3], totals[4], totals[5], totals[6], totals[7], totals[8], totals[9], totals[10], totals[11], totals[12], totals[13], totals[14])
```

```python
import jax
import jax.numpy as jnp
from jax import lax
from jax.experimental import pallas as pl
from jax.experimental.pallas import tpu as pltpu
from jax.sharding import Mesh
from jax.sharding import PartitionSpec as P

HD = 64
norm_eps = 1e-06
bf16 = jnp.bfloat16
f32 = jnp.float32
SCALE = HD ** (-0.5)


def shift(v, axis, by):
    return lax.ppermute(v, axis, [(i, (i + by) % 4) for i in range(4)])


def gather4(v, axis):
    far = shift(v, axis, 2)
    return [v, shift(v, axis, 1), shift(v, axis, 3), far]


def scatter4(parts, axis):
    far = shift(parts[3], axis, 2)
    return [parts[0], shift(parts[1], axis, 3), shift(parts[2], axis, 1), far]


def sum4(parts):
    a, b, c, d = [p.astype(f32) for p in parts]
    return (a + b) + (c + d)


def swap_core(v):
    return lax.ppermute(v, "section", [(0, 1), (1, 0)])


def swap_pair(v):
    return lax.ppermute(v, "row", [(0, 1), (1, 0), (2, 3), (3, 2)])


def gather_tokens(rows):
    return jnp.concatenate(gather4(rows, "z"), axis=0)


def scatter_tokens(partial):
    low = partial.astype(bf16)
    n = low.shape[0] // 4
    return sum4(scatter4([low[i * n : (i + 1) * n] for i in range(4)], "z"))


def dot(a, b):
    return jnp.dot(a, b, preferred_element_type=f32)


def dot_t(a, b):
    return lax.dot_general(a, b, (((1,), (1,)), ((), ())), preferred_element_type=f32)


def t_dot(a, b):
    return lax.dot_general(a, b, (((0,), (0,)), ((), ())), preferred_element_type=f32)


def norm_local(features, gain, bias):
    center = jnp.mean(features, axis=-1, keepdims=True)
    offset = features - center
    spread = jnp.mean(offset * offset, axis=-1, keepdims=True)
    inverse = lax.rsqrt(spread + norm_eps)
    scaled = offset * inverse
    return scaled * gain + bias, scaled, inverse


def norm_back(upstream, scaled, inverse, gain):
    weighted = upstream * gain
    first = jnp.mean(weighted, axis=-1, keepdims=True)
    second = jnp.mean(weighted * scaled, axis=-1, keepdims=True)
    result = inverse * (weighted - first - scaled * second)
    return result, jnp.sum(upstream * scaled, axis=0), jnp.sum(upstream, axis=0)


def gelu_both(v):
    cdf = 0.5 * (1.0 + lax.erf(v * (0.5**0.5)))
    density = jnp.exp(-0.5 * v * v) * 0.3989422804014327
    return (v * cdf).astype(bf16), cdf + v * density


def attend_kernel(q_ref, own_ref, core_ref, pair_ref, both_ref, o_ref, lt_ref):
    q = q_ref[...]
    kv = jnp.concatenate([own_ref[...], core_ref[...], pair_ref[...], both_ref[...]], axis=0)
    s = dot_t(q, kv) * SCALE
    peak = jnp.max(s, axis=-1, keepdims=True)
    raised = jnp.exp(s - peak)
    total = jnp.sum(raised, axis=-1, keepdims=True)
    low = (raised * (1.0 / total)).astype(bf16)
    o = dot(low, kv)
    upper = lax.broadcasted_iota(jnp.int32, o.shape, 1) >= HD
    o_ref[...] = jnp.where(upper, o, 0.0).astype(bf16)
    lt_ref[...] = jnp.broadcast_to(peak + jnp.log(total), lt_ref.shape)


def attend(q, kvs):
    tokens, width = q.shape
    spec = pl.BlockSpec((tokens, 128), lambda h: (0, h))
    return pl.pallas_call(
        attend_kernel,
        grid=(width // 128,),
        in_specs=[spec] * 5,
        out_specs=[spec, spec],
        out_shape=[
            jax.ShapeDtypeStruct((tokens, width), bf16),
            jax.ShapeDtypeStruct((tokens, width), f32),
        ],
        compiler_params=pltpu.CompilerParams(vmem_limit_bytes=32 * 2**20),
        cost_estimate=pl.CostEstimate(flops=4 * 2 * 2 * 256 * 1024 * 128, bytes_accessed=2**21, transcendentals=2**20),
    )(q, *kvs)


def attend_back_kernel(
    q_ref, own_ref, core_ref, pair_ref, both_ref, g_ref, lt_ref, dq_ref, down_ref, dcore_ref, dpair_ref, dboth_ref
):
    q = q_ref[...]
    n = q.shape[0]
    upper = lax.broadcasted_iota(jnp.int32, q.shape, 1) >= HD
    g = jnp.where(upper, g_ref[...], jnp.zeros_like(q))
    kv = jnp.concatenate([own_ref[...], core_ref[...], pair_ref[...], both_ref[...]], axis=0)
    s = dot_t(q, kv) * SCALE
    probs = jnp.exp(s - lt_ref[:, 0:1])
    grad_probs = dot_t(g, kv)
    along = jnp.sum(probs * grad_probs, axis=-1, keepdims=True)
    ds = (probs * (grad_probs - along)).astype(bf16)
    low = probs.astype(bf16)
    dq = dot(ds, kv) * SCALE
    dq_ref[...] = jnp.where(upper, 0.0, dq).astype(bf16)
    dkv = t_dot(ds, q) * SCALE + t_dot(low, g)
    down_ref[...] = dkv[0:n].astype(down_ref.dtype)
    dcore_ref[...] = dkv[n : 2 * n].astype(dcore_ref.dtype)
    dpair_ref[...] = dkv[2 * n : 3 * n].astype(dpair_ref.dtype)
    dboth_ref[...] = dkv[3 * n :].astype(dboth_ref.dtype)


def attend_back(q, kvs, g, lt):
    tokens, width = q.shape
    spec = pl.BlockSpec((tokens, 128), lambda h: (0, h))
    return pl.pallas_call(
        attend_back_kernel,
        grid=(width // 128,),
        in_specs=[spec] * 7,
        out_specs=[spec] * 5,
        out_shape=[
            jax.ShapeDtypeStruct((tokens, width), bf16),
            jax.ShapeDtypeStruct((tokens, width), f32),
            jax.ShapeDtypeStruct((tokens, width), bf16),
            jax.ShapeDtypeStruct((tokens, width), f32),
            jax.ShapeDtypeStruct((tokens, width), bf16),
        ],
        compiler_params=pltpu.CompilerParams(vmem_limit_bytes=40 * 2**20),
        cost_estimate=pl.CostEstimate(flops=4 * 5 * 2 * 256 * 1024 * 128, bytes_accessed=2**22, transcendentals=2**20),
    )(q, *kvs, g, lt)


def forward(u, w):
    vec = w["vec"]
    lower = (jnp.arange(512) % 128) < HD
    n1, scaled1, inv1 = norm_local(u, vec[0], vec[1])
    x = gather_tokens(n1.astype(bf16))
    kv = (dot(x, w["kv"]) + w["kv_bias"]).astype(bf16)
    q = (jnp.where(lower, dot(x, w["qp"]), 0.0) + w["q_bias"]).astype(bf16)
    kv_pair = swap_pair(kv)
    kvs = (kv, swap_core(kv), kv_pair, swap_core(kv_pair))
    o, lt = attend(q, kvs)
    attended = scatter_tokens(dot_t(o, w["qp"])) + vec[2]
    hidden = u + vec[3] * attended
    n2, scaled2, inv2 = norm_local(hidden, vec[4], vec[5])
    x2 = gather_tokens(n2.astype(bf16))
    a_own, da_own = gelu_both(dot(x2, w["in_own"]) + w["in_bias_own"])
    a_oth, da_oth = gelu_both(dot(x2, w["in_oth"]) + w["in_bias_oth"])
    contracted = scatter_tokens(dot_t(a_own, w["out_own"]) + dot_t(a_oth, w["out_oth"])) + vec[6]
    out = hidden + vec[7] * contracted
    return out, (scaled1, inv1, x, kvs, q, o, lt, attended, scaled2, inv2, x2, a_own, da_own, a_oth, da_oth, contracted)


def both_cores(mine, sent):
    return jnp.concatenate([mine, swap_core(sent)], axis=0)


def backward(g, saved, w, first):
    scaled1, inv1, x, kvs, q, o, lt, attended, scaled2, inv2, x2, a_own, da_own, a_oth, da_oth, contracted = saved
    vec = w["vec"]
    grad_mlp_scale = jnp.sum(g * contracted, axis=0)
    gc = (g * vec[7]).astype(bf16)
    grad_outer_bias = jnp.sum(gc.astype(f32), axis=0)
    gcs = gather_tokens(gc)
    ge_own = (dot(gcs, w["out_own"]) * da_own).astype(bf16)
    ge_oth = (dot(gcs, w["out_oth"]) * da_oth).astype(bf16)
    grad_second = scatter_tokens(dot_t(ge_own, w["in_own"]) + dot_t(ge_oth, w["in_oth"]))
    d_out = t_dot(both_cores(gcs, gcs), both_cores(a_own, a_oth)).astype(bf16)
    ge_both = both_cores(ge_own, ge_oth)
    d_in = t_dot(both_cores(x2, x2), ge_both).astype(bf16)
    in_bias_sum = jnp.sum(ge_both.astype(f32), axis=0)
    back, grad_gain2, grad_bias2 = norm_back(grad_second, scaled2, inv2, vec[4])
    grad_hidden = g + back
    grad_attn_scale = jnp.sum(grad_hidden * attended, axis=0)
    ga = (grad_hidden * vec[3]).astype(bf16)
    grad_proj_bias = jnp.sum(ga.astype(f32), axis=0)
    gas = gather_tokens(ga)
    gz = dot(gas, w["qp"]).astype(bf16)
    dq, d_own, d_core, d_pair, d_both = attend_back(q, kvs, gz, lt)
    pair_sum = (d_pair + swap_core(d_both).astype(f32)).astype(bf16)
    dkv = (d_own + swap_core(d_core).astype(f32) + swap_pair(pair_sum).astype(f32)).astype(bf16)
    grad_normed = scatter_tokens(dot_t(dkv, w["kv"]) + dot_t(dq, w["qp"]))
    m1 = both_cores(jnp.where(first, dkv, dq), jnp.where(first, dq, dkv))
    m2 = jnp.where(first, jnp.zeros((), bf16), both_cores(o, o))
    d_att = (t_dot(both_cores(x, x), m1) + t_dot(both_cores(gas, gas), m2)).astype(bf16)
    att_bias_sum = jnp.sum(m1.astype(f32), axis=0)
    back, grad_gain1, grad_bias1 = norm_back(grad_normed, scaled1, inv1, vec[0])
    grad_u = grad_hidden + back
    rows = jnp.stack(
        [grad_gain1, grad_bias1, grad_proj_bias, grad_attn_scale, grad_gain2, grad_bias2, grad_outer_bias, grad_mlp_scale]
    )
    cols = jnp.concatenate([att_bias_sum.reshape(4, 128), in_bias_sum.reshape(4, 128)], axis=1)
    return grad_u, (d_att, d_in, d_out), rows, cols


def gather_block(block):
    rows = jnp.concatenate(gather4(block, "row"), axis=0)
    return gather4(rows, "x")


def side_by_side(tiles, at, width):
    return jnp.concatenate([t[:, at : at + width] for t in tiles], axis=1)


def layer_weights(half_att, half_ffn, vec_y, vec_x, first):
    att = side_by_side(gather_block(half_att), 0, 128)
    att_far = swap_core(att)
    tiles = gather_block(half_ffn)
    in_own, out_own = side_by_side(tiles, 0, 128), side_by_side(tiles, 128, 128)
    zeros = jnp.zeros((HD,), f32)
    kv_bias = jnp.concatenate([t for v in vec_x for t in (zeros, v[HD : 2 * HD])])
    q_bias = jnp.concatenate([t for v in vec_x for t in (v[:HD], zeros)])
    low = jnp.concatenate([v[128:256] for v in vec_x])
    high = jnp.concatenate([v[256:384] for v in vec_x])
    return {
        "vec": vec_y,
        "kv": jnp.where(first, att, att_far),
        "qp": jnp.where(first, att_far, att),
        "in_own": in_own,
        "out_own": out_own,
        "in_oth": swap_core(in_own),
        "out_oth": swap_core(out_own),
        "kv_bias": kv_bias,
        "q_bias": q_bias,
        "in_bias_own": jnp.where(first, low, high),
        "in_bias_oth": jnp.where(first, high, low),
    }


def reduce_block(d, count):
    parts = [jnp.concatenate([m[:, i * 128 : (i + 1) * 128] for m in d], axis=1) for i in range(4)]
    summed = sum4(scatter4(parts, "x")).astype(bf16)
    n = summed.shape[0] // 4
    return sum4(scatter4([summed[i * n : (i + 1) * n] for i in range(4)], "row"))


def local(
    block_input,
    cotangent,
    images_used,
    norm1_gain,
    norm1_bias,
    qkv_weight,
    query_bias,
    value_bias,
    proj_weight,
    proj_bias,
    attn_scale,
    norm2_gain,
    norm2_bias,
    inner_weight,
    inner_bias,
    outer_weight,
    outer_bias,
    mlp_scale,
):
    first = lax.axis_index("section") == 0
    y = lax.axis_index("row")

    qkv = qkv_weight[0]
    half0_att = qkv[:, HD:]
    half1_att = jnp.concatenate([qkv[:, :HD], proj_weight[0].T], axis=1)
    outer_t = outer_weight[0].T
    half0_ffn = jnp.concatenate([inner_weight[0][:, :128], outer_t[:, :128]], axis=1)
    half1_ffn = jnp.concatenate([inner_weight[0][:, 128:], outer_t[:, 128:]], axis=1)

    def split_layers(h0, h1):
        kept, got = jnp.where(first, h0, h1), swap_core(jnp.where(first, h1, h0))
        return jnp.where(first, kept, got), jnp.where(first, got, kept)

    att0, att1 = split_layers(half0_att, half1_att)
    ffn0, ffn1 = split_layers(half0_ffn, half1_ffn)

    def both_layers(own):
        got = swap_core(own)
        return jnp.stack([jnp.where(first, own, got), jnp.where(first, got, own)])

    vec_y = both_layers(
        jnp.concatenate(
            [norm1_gain, norm1_bias, proj_bias, attn_scale, norm2_gain, norm2_bias, outer_bias, mlp_scale], axis=0
        )
    )
    vec_x = both_layers(jnp.concatenate([query_bias[0], value_bias[0], inner_bias[0]]))
    vec_y = jnp.concatenate(gather4(vec_y, "row"), axis=2)
    vec_x = gather4(vec_x, "x")

    paired = jnp.stack([block_input, cotangent]).reshape(2, 4, 2, 64, 256)
    paired = jnp.where(first, paired[:, :, 0], paired[:, :, 1])
    chunk = [lax.dynamic_index_in_dim(paired, (y + k) % 4, 1, keepdims=False) for k in (0, 3, 1, 2)]
    got = scatter4(chunk, "row")
    tokens = jnp.concatenate([got[0], got[2], got[1], got[3]], axis=2).astype(f32)

    w0 = layer_weights(att0, ffn0, vec_y[0], [v[0] for v in vec_x], first)
    w1 = layer_weights(att1, ffn1, vec_y[1], [v[1] for v in vec_x], first)

    used = jnp.where(y < 2, images_used[0], images_used[1])
    live = (lax.axis_index("x") < used).astype(f32)

    out0, saved0 = forward(tokens[0], w0)
    out1, saved1 = forward(out0.astype(bf16).astype(f32), w1)
    final = (live * out1).astype(bf16)
    back1, d1, rows1, cols1 = backward(live * tokens[1], saved1, w1, first)
    back0, d0, rows0, cols0 = backward(back1.astype(bf16).astype(f32), saved0, w0, first)
    grad_in = back0.astype(bf16)

    own = jnp.where(first, grad_in, final)
    got = swap_core(jnp.where(first, final, grad_in))
    edge = jnp.concatenate([jnp.where(first, own, got), jnp.where(first, got, own)], axis=0)
    got = scatter4([edge[:, i * 256 : (i + 1) * 256] for i in range(4)], "row")
    edge = jnp.stack([got[0], got[1], got[3], got[2]])
    edge = lax.dynamic_slice_in_dim(jnp.concatenate([edge, edge]), (4 - y) % 4, 4, 0)
    edge = edge.reshape(1, 2, 256, 256).astype(f32)

    def own_layer(l0, l1):
        got = swap_core(jnp.where(first, l1, l0))
        mine = jnp.where(first, l0, l1)
        return jnp.where(first, mine, got), jnp.where(first, got, mine)

    d_ffn = own_layer(*[reduce_block(d[1:], 2).astype(bf16) for d in (d0, d1)])
    d_att = own_layer(*[reduce_block(d[:1], 1).astype(bf16) for d in (d0, d1)])
    h0, h1 = [h.astype(f32) for h in d_att]
    grad_qkv = jnp.concatenate([h1[:, :HD], h0], axis=1)
    grad_proj = h1[:, HD:].T
    h0, h1 = [h.astype(f32) for h in d_ffn]
    grad_inner = jnp.concatenate([h0[:, :128], h1[:, :128]], axis=1)
    grad_outer = jnp.concatenate([h0[:, 128:], h1[:, 128:]], axis=1).T

    cols = jnp.stack([cols0, cols1], axis=1)
    cols = sum4(scatter4([cols[i] for i in range(4)], "x"))
    cols = sum4(gather4(cols, "row"))
    h0, h1 = own_layer(cols[0], cols[1])
    grad_query_bias, grad_value_bias = h1[:HD], h0[HD:128]
    grad_inner_bias = jnp.concatenate([h0[128:], h1[128:]])

    rows = jnp.where(first, rows0, rows1) + swap_core(jnp.where(first, rows1, rows0))
    rows = sum4(scatter4([rows[:, i * 256 : (i + 1) * 256] for i in range(4)], "row"))
    rows = sum4(gather4(rows, "x"))
    rows = sum4(gather4(rows, "z"))

    return (
        edge,
        rows[0][None],
        rows[1][None],
        grad_qkv[None],
        grad_query_bias[None],
        grad_value_bias[None],
        grad_proj[None],
        rows[2][None],
        rows[3][None],
        rows[4][None],
        rows[5][None],
        grad_inner[None],
        grad_inner_bias[None],
        grad_outer[None],
        rows[6][None],
        rows[7][None],
    )


def solution(mesh):
    grid = Mesh(mesh.devices.reshape(2, 4, 4, 4), ("section", "row", "x", "z"))
    col = ("x", "z")
    by_row = P("section", "row")
    by_col = P("section", col)
    matrix = P("section", "row", col)
    matrix_t = P("section", col, "row")
    return jax.shard_map(
        local,
        mesh=grid,
        in_specs=(
            P(None, col, "row"),
            P(None, col, "row"),
            P(),
            by_row,
            by_row,
            matrix,
            by_col,
            by_col,
            matrix_t,
            by_row,
            by_row,
            by_row,
            by_row,
            matrix,
            by_col,
            matrix_t,
            by_row,
            by_row,
        ),
        out_specs=(
            P("section", None, col, "row"),
            by_row,
            by_row,
            matrix,
            by_col,
            by_col,
            matrix_t,
            by_row,
            by_row,
            by_row,
            by_row,
            matrix,
            by_col,
            matrix_t,
            by_row,
            by_row,
        ),
        check_vma=False,
    )
```

```python
import functools

import jax
import jax.numpy as jnp
from jax import lax
from jax.experimental import pallas as pl
from jax.experimental.pallas import tpu as pltpu
from jax.sharding import Mesh
from jax.sharding import PartitionSpec as P

HD = 64
norm_eps = 1e-06
bf16 = jnp.bfloat16
f32 = jnp.float32
SCALE = HD ** (-0.5)


def shift(v, axis, by):
    return lax.ppermute(v, axis, [(i, (i + by) % 4) for i in range(4)])


def gather4(v, axis):
    far = shift(v, axis, 2)
    return [v, shift(v, axis, 1), shift(v, axis, 3), far]


def scatter4(parts, axis):
    far = shift(parts[3], axis, 2)
    return [parts[0], shift(parts[1], axis, 3), shift(parts[2], axis, 1), far]


def sum4(parts):
    a, b, c, d = [p.astype(f32) for p in parts]
    return (a + b) + (c + d)


def swap_core(v):
    return lax.ppermute(v, "section", [(0, 1), (1, 0)])


def swap_pair(v):
    return lax.ppermute(v, "row", [(0, 1), (1, 0), (2, 3), (3, 2)])


def gather_tokens(rows):
    return jnp.concatenate(gather4(rows, "z"), axis=0)


def scatter_tokens(partial):
    low = partial.astype(bf16)
    n = low.shape[0] // 4
    return sum4(scatter4([low[i * n : (i + 1) * n] for i in range(4)], "z"))


def dot(a, b):
    return jnp.dot(a, b, preferred_element_type=f32)


def dot_t(a, b):
    return lax.dot_general(a, b, (((1,), (1,)), ((), ())), preferred_element_type=f32)


def t_dot(a, b):
    return lax.dot_general(a, b, (((0,), (0,)), ((), ())), preferred_element_type=f32)


def norm_local(features, gain, bias):
    center = jnp.mean(features, axis=-1, keepdims=True)
    offset = features - center
    spread = jnp.mean(offset * offset, axis=-1, keepdims=True)
    inverse = lax.rsqrt(spread + norm_eps)
    scaled = offset * inverse
    return scaled * gain + bias, scaled, inverse


def norm_back(upstream, scaled, inverse, gain):
    weighted = upstream * gain
    first = jnp.mean(weighted, axis=-1, keepdims=True)
    second = jnp.mean(weighted * scaled, axis=-1, keepdims=True)
    return inverse * (weighted - first - scaled * second)


def gelu_both(v):
    cdf = 0.5 * (1.0 + lax.erf(v * (0.5**0.5)))
    density = jnp.exp(-0.5 * v * v) * 0.3989422804014327
    return (v * cdf).astype(bf16), cdf + v * density


def attend_kernel(q_ref, own_ref, core_ref, pair_ref, both_ref, o_ref, lt_ref):
    q = q_ref[...]
    kv = jnp.concatenate([own_ref[...], core_ref[...], pair_ref[...], both_ref[...]], axis=0)
    s = dot_t(q, kv) * SCALE
    peak = jnp.max(s, axis=-1, keepdims=True)
    raised = jnp.exp(s - peak)
    total = jnp.sum(raised, axis=-1, keepdims=True)
    low = (raised * (1.0 / total)).astype(bf16)
    o = dot(low, kv)
    upper = lax.broadcasted_iota(jnp.int32, o.shape, 1) >= HD
    o_ref[...] = jnp.where(upper, o, 0.0).astype(bf16)
    lt_ref[...] = jnp.broadcast_to(peak + jnp.log(total), lt_ref.shape)


def attend(q, kvs):
    tokens, width = q.shape
    spec = pl.BlockSpec((tokens, 128), lambda h: (0, h))
    return pl.pallas_call(
        attend_kernel,
        grid=(width // 128,),
        in_specs=[spec] * 5,
        out_specs=[spec, spec],
        out_shape=[
            jax.ShapeDtypeStruct((tokens, width), bf16),
            jax.ShapeDtypeStruct((tokens, width), f32),
        ],
        compiler_params=pltpu.CompilerParams(vmem_limit_bytes=32 * 2**20),
        cost_estimate=pl.CostEstimate(flops=4 * 2 * 2 * 256 * 1024 * 128, bytes_accessed=2**21, transcendentals=2**20),
    )(q, *kvs)


def attend_back_kernel(
    q_ref, own_ref, core_ref, pair_ref, both_ref, g_ref, lt_ref, dq_ref, down_ref, dcore_ref, dpair_ref, dboth_ref
):
    q = q_ref[...]
    n = q.shape[0]
    upper = lax.broadcasted_iota(jnp.int32, q.shape, 1) >= HD
    g = jnp.where(upper, g_ref[...], jnp.zeros_like(q))
    kv = jnp.concatenate([own_ref[...], core_ref[...], pair_ref[...], both_ref[...]], axis=0)
    s = dot_t(q, kv) * SCALE
    probs = jnp.exp(s - lt_ref[:, 0:1])
    grad_probs = dot_t(g, kv)
    along = jnp.sum(probs * grad_probs, axis=-1, keepdims=True)
    ds = (probs * (grad_probs - along)).astype(bf16)
    low = probs.astype(bf16)
    dq = dot(ds, kv) * SCALE
    dq_ref[...] = jnp.where(upper, 0.0, dq).astype(bf16)
    dkv = t_dot(ds, q) * SCALE + t_dot(low, g)
    down_ref[...] = dkv[0:n].astype(down_ref.dtype)
    dcore_ref[...] = dkv[n : 2 * n].astype(dcore_ref.dtype)
    dpair_ref[...] = dkv[2 * n : 3 * n].astype(dpair_ref.dtype)
    dboth_ref[...] = dkv[3 * n :].astype(dboth_ref.dtype)


def attend_back(q, kvs, g, lt):
    tokens, width = q.shape
    spec = pl.BlockSpec((tokens, 128), lambda h: (0, h))
    return pl.pallas_call(
        attend_back_kernel,
        grid=(width // 128,),
        in_specs=[spec] * 7,
        out_specs=[spec] * 5,
        out_shape=[
            jax.ShapeDtypeStruct((tokens, width), bf16),
            jax.ShapeDtypeStruct((tokens, width), f32),
            jax.ShapeDtypeStruct((tokens, width), bf16),
            jax.ShapeDtypeStruct((tokens, width), f32),
            jax.ShapeDtypeStruct((tokens, width), bf16),
        ],
        compiler_params=pltpu.CompilerParams(vmem_limit_bytes=40 * 2**20),
        cost_estimate=pl.CostEstimate(flops=4 * 5 * 2 * 256 * 1024 * 128, bytes_accessed=2**22, transcendentals=2**20),
    )(q, *kvs, g, lt)


def store_sums(out_ref, at, a, b):
    sums = jnp.sum(a[...].astype(f32), axis=0, keepdims=True) + jnp.sum(b[...].astype(f32), axis=0, keepdims=True)
    for i in range(4):
        row = jnp.concatenate([sums[:, i * 128 : (i + 1) * 128], jnp.zeros((1, 128), f32)], axis=1)
        out_ref[i, 0, at : at + 16, :] = jnp.broadcast_to(row, (16, 256)).astype(bf16)


def store_tiles(out_ref, at, d):
    for i in range(4):
        out_ref[i, 0, at : at + 128, :] = d[i * 128 : (i + 1) * 128].astype(bf16)


def ffn_part(out_ref, at, ge, ge_far, act, act_far, x, x_far, g, g_far):
    store_tiles(out_ref, at, t_dot(ge[...], x[...]) + t_dot(ge_far[...], x_far[...]))
    store_tiles(out_ref, at + 128, t_dot(act[...], g[...]) + t_dot(act_far[...], g_far[...]))
    store_sums(out_ref, at + 256, ge, ge_far)


def att_part(out_ref, at, m, m_far, o, o_far, x, x_far, g, g_far, mask_ref):
    d_proj = t_dot(o[...], g[...]) + t_dot(o_far[...], g_far[...])
    store_tiles(out_ref, at, t_dot(m[...], x[...]) + t_dot(m_far[...], x_far[...]) + mask_ref[...] * d_proj)
    store_sums(out_ref, at + 128, m, m_far)


def ffn_grads_kernel(*refs):
    ffn_part(refs[-1], 0, *refs[:8])


def att_grads_kernel(*refs):
    att_part(refs[-1], 0, *refs[:9])


def layer_grads_kernel(*refs):
    ffn_part(refs[-1], 0, *refs[:8])
    att_part(refs[-1], 272, *refs[8:17])


def block_grads(kernel, rows, operands):
    specs = []
    for v in operands:
        if v.shape[1] == 1024:
            specs.append(pl.BlockSpec((v.shape[0], 256), lambda j: (0, j)))
        else:
            specs.append(pl.BlockSpec(v.shape, lambda j: (0, 0)))
    return pl.pallas_call(
        kernel,
        grid=(4,),
        in_specs=specs,
        out_specs=pl.BlockSpec((4, 1, rows, 256), lambda j: (0, j, 0, 0)),
        out_shape=jax.ShapeDtypeStruct((4, 4, rows, 256), bf16),
        compiler_params=pltpu.CompilerParams(vmem_limit_bytes=60 * 2**20),
        cost_estimate=pl.CostEstimate(flops=rows * 2**24, bytes_accessed=8 * 2**20, transcendentals=0),
    )(*operands)


def assemble_kernel(first_ref, mine_ref, got_ref, qkv, qb, vb, proj, inner, ib, outer, rows):
    mine, got = mine_ref[...].astype(f32), got_ref[...].astype(f32)
    first = first_ref[0] == 0
    h0, h1 = jnp.where(first, mine, got), jnp.where(first, got, mine)
    inner[...] = jnp.concatenate([h0[0:128], h1[0:128]], axis=0).T
    outer[...] = jnp.concatenate([h0[128:256], h1[128:256]], axis=0)
    ib[...] = jnp.concatenate([h0[256:257, :128], h1[256:257, :128]], axis=1)
    qkv[...] = jnp.concatenate([h1[272:336], h0[272:400]], axis=0).T
    proj[...] = h1[336:400]
    qb[...] = h1[400:401, :HD]
    vb[...] = h0[400:401, HD:128]
    rows[...] = h0[416:424] + h1[416:424]


def assemble(first, mine, got):
    shapes = [(256, 192), (1, HD), (1, HD), (64, 256), (256, 256), (1, 256), (256, 256), (8, 256)]
    vmem = pl.BlockSpec(memory_space=pltpu.VMEM)
    return pl.pallas_call(
        assemble_kernel,
        in_specs=[pl.BlockSpec(memory_space=pltpu.SMEM), vmem, vmem],
        out_shape=[jax.ShapeDtypeStruct(v, f32) for v in shapes],
        compiler_params=pltpu.CompilerParams(vmem_limit_bytes=32 * 2**20),
    )(jnp.where(first, 0, 1).astype(jnp.int32).reshape(1), mine, got)


def rows_kernel(direct, a, b, vec, ga, gh, att, gs, n2, gc, g, con, out_ref):
    left = a[...]
    right = b[...] if direct else (b[...].astype(f32) - vec[1:2, :]) * (1.0 / vec[0:1, :])
    out_ref[0:1, :] = jnp.sum(left * right, axis=0, keepdims=True)
    out_ref[1:2, :] = jnp.sum(left, axis=0, keepdims=True)
    out_ref[2:3, :] = jnp.sum(ga[...].astype(f32), axis=0, keepdims=True)
    out_ref[3:4, :] = jnp.sum(gh[...] * att[...], axis=0, keepdims=True)
    out_ref[4:5, :] = jnp.sum(gs[...] * n2[...], axis=0, keepdims=True)
    out_ref[5:6, :] = jnp.sum(gs[...], axis=0, keepdims=True)
    out_ref[6:7, :] = jnp.sum(gc[...].astype(f32), axis=0, keepdims=True)
    out_ref[7:8, :] = jnp.sum(g[...] * con[...], axis=0, keepdims=True)


def row_sums(direct, *arrays):
    return pl.pallas_call(
        functools.partial(rows_kernel, direct),
        out_shape=jax.ShapeDtypeStruct((8, 1024), f32),
        compiler_params=pltpu.CompilerParams(vmem_limit_bytes=32 * 2**20),
        cost_estimate=pl.CostEstimate(flops=2**21, bytes_accessed=4 * 2**20, transcendentals=0),
    )(*arrays)


def forward(u, w, beside=None, late=False):
    vec = w["vec"]
    lower = (jnp.arange(512) % 128) < HD
    n1, scaled1, inv1 = norm_local(u, vec[0], vec[1])
    x = gather_tokens(n1.astype(bf16))
    if "att" in w:
        att, x = lax.optimization_barrier((w["att"], x))
        w.update(att_weights(att, w["first"]))
    kv = (dot(x, w["kv"]) + w["kv_bias"]).astype(bf16)
    if beside is not None:
        kv, beside = lax.optimization_barrier((kv, beside))
    kv_pair = swap_pair(kv)
    q = (jnp.where(lower, dot(x, w["qp"]), 0.0) + w["q_bias"]).astype(bf16)
    if beside is not None:
        kv_pair, beside = lax.optimization_barrier((kv_pair, (beside, gather_tokens(beside))))
    kvs = (kv, swap_core(kv), kv_pair, swap_core(kv_pair))
    o, lt = attend(q, kvs)
    attended = scatter_tokens(dot_t(o, w["qp"])) + vec[2]
    hidden = u + vec[3] * attended
    n2, scaled2, inv2 = norm_local(hidden, vec[4], vec[5])
    x2 = gather_tokens(n2.astype(bf16))
    a_own, da_own = gelu_both(dot(x2, w["in_own"]) + w["in_bias_own"])
    a_oth, da_oth = gelu_both(dot(x2, w["in_oth"]) + w["in_bias_oth"])
    partial = (dot_t(a_own, w["out_own"]) + dot_t(a_oth, w["out_oth"])).astype(bf16)
    if not late:
        contracted = scatter_tokens(partial) + vec[6]
    else:

        def contracted(after):
            late, _ = lax.optimization_barrier((partial, after))
            return scatter_tokens(late) + vec[6]

    one, two = (x, kvs, q, o, lt), (scaled2, inv2, x2, a_own, da_own, a_oth, da_oth)
    return hidden, contracted, (scaled1, inv1, attended), one, two, beside


def reduce_x(blocks):
    return sum4(scatter4([blocks[i] for i in range(4)], "x")).astype(bf16)


def reduce_y(blocks):
    return sum4(scatter4(to_slots(blocks), "row")).astype(bf16)


def to_slots(blocks):
    y = lax.axis_index("row")
    return [lax.dynamic_index_in_dim(blocks, (y + k) % 4, 0, keepdims=False) for k in (0, 3, 1, 2)]


def in_order(parts):
    y = lax.axis_index("row")
    stacked = jnp.stack([parts[0], parts[1], parts[3], parts[2]])
    return lax.dynamic_slice_in_dim(jnp.concatenate([stacked, stacked]), (4 - y) % 4, 4, 0)


def backward_ffn(g, gc, gcs, saved, w):
    scaled2, inv2, x2, a_own, da_own, a_oth, da_oth = saved
    ge_own = (dot(gcs, w["out_own"]) * da_own).astype(bf16)
    ge_oth = (dot(gcs, w["out_oth"]) * da_oth).astype(bf16)
    grad_second = scatter_tokens(dot_t(ge_own, w["in_own"]) + dot_t(ge_oth, w["in_oth"]))
    grad_hidden = g + norm_back(grad_second, scaled2, inv2, w["vec"][4])
    ga = (grad_hidden * w["vec"][3]).astype(bf16)
    operands = (ge_own, swap_core(ge_oth), a_own, swap_core(a_oth), x2, swap_core(x2), gcs, swap_core(gcs))
    return grad_hidden, grad_second, ga, operands


def backward_att(gas, saved, w):
    x, kvs, q, o, lt = saved
    gz = dot(gas, w["qp"]).astype(bf16)
    dq, d_own, d_core, d_pair, d_both = attend_back(q, kvs, gz, lt)
    pair_sum = (d_pair + swap_core(d_both).astype(f32)).astype(bf16)
    near = d_own + swap_core(d_core).astype(f32)
    return dq, near, pair_sum


def att_operands(first, dkv, dq, gas, saved):
    x, _, _, o, _ = saved
    return (
        jnp.where(first, dkv, dq),
        swap_core(jnp.where(first, dq, dkv)),
        o,
        swap_core(o),
        x,
        swap_core(x),
        gas,
        swap_core(gas),
        jnp.full((1, 256), jnp.where(first, 0.0, 1.0), f32),
    )


def rows_of(tiles, n):
    return jnp.concatenate([t[:, :n].reshape(-1, t.shape[2]) for t in tiles], axis=1)


def tiles_gathered(half):
    tiles = lax.all_gather(half, ("x", "row"), axis=0, tiled=True).reshape(4, 4, *half.shape)
    return [tiles[i] for i in range(4)]


def split(v):
    high = v.astype(bf16).astype(f32)
    return high, v - high


def cut_weights_kernel(first_ref, qkv_ref, proj_ref, inner_ref, outer_ref, qb, vb, ib, *refs):
    vectors, kept_ref, sent_ref = refs
    mine = first_ref[0] == 0
    qkv = qkv_ref[...].astype(f32)
    outer_t = outer_ref[...].astype(f32).T
    inner = inner_ref[...].astype(f32)
    kv = qkv[:, HD:]
    qp = jnp.concatenate([qkv[:, :HD], proj_ref[...].astype(f32).T], axis=1)
    none = jnp.zeros((1, HD), f32)
    bias0 = jnp.concatenate([none, vb[...], ib[:, :128], none, none], axis=1)
    bias1 = jnp.concatenate([qb[...], none, ib[:, 128:], none, none], axis=1)
    pad = jnp.zeros((14, 384), f32)
    half0 = [jnp.concatenate([kv, inner[:, :128], outer_t[:, :128]], axis=1), *split(bias0), pad]
    half1 = [jnp.concatenate([qp, inner[:, 128:], outer_t[:, 128:]], axis=1), *split(bias1), pad]
    vec = jnp.concatenate(split(vectors[...]), axis=0)
    vec = jnp.concatenate([vec, jnp.zeros((16, 128), f32)], axis=1)
    half0 = jnp.concatenate([*half0, vec], axis=0)
    half1 = jnp.concatenate([*half1, vec], axis=0)
    kept_ref[...] = jnp.where(mine, half0, half1).astype(bf16)
    sent_ref[...] = jnp.where(mine, half1, half0).astype(bf16)


def cut_weights(first, *arrays):
    place = pl.BlockSpec(memory_space=pltpu.SMEM)
    return pl.pallas_call(
        cut_weights_kernel,
        in_specs=[place] + [pl.BlockSpec(memory_space=pltpu.VMEM)] * len(arrays),
        out_shape=[jax.ShapeDtypeStruct((288, 384), bf16)] * 2,
        compiler_params=pltpu.CompilerParams(vmem_limit_bytes=60 * 2**20),
    )(jnp.where(first, 0, 1).astype(jnp.int32).reshape(1), *arrays)


def joined(rows):
    return rows[0].astype(f32) + rows[1].astype(f32)


def att_weights(att, first):
    far = swap_core(att)
    kv, qp = jnp.where(first, att, far), jnp.where(first, far, att)
    return {"kv": kv[:1024], "qp": qp[:1024], "kv_bias": joined(kv[1024:]), "q_bias": joined(qp[1024:])}


def ffn_weights(tiles, at):
    in_own = rows_of([t[:, :, at : at + 128] for t in tiles], 256)
    out_own = rows_of([t[:, :, at + 128 : at + 256] for t in tiles], 256)
    bias = jnp.concatenate([joined(t[0, 256:258, at : at + 128]) for t in tiles])
    return {
        "in_own": in_own,
        "out_own": out_own,
        "in_oth": swap_core(in_own),
        "out_oth": swap_core(out_own),
        "in_bias_own": bias,
        "in_bias_oth": swap_core(bias),
    }


def sum_over(blocks, axis):
    rows = blocks.reshape(-1, blocks.shape[-1])
    return lax.psum_scatter(rows, axis, scatter_dimension=0, tiled=True).reshape(blocks.shape[1:])


def local(
    block_input,
    cotangent,
    images_used,
    norm1_gain,
    norm1_bias,
    qkv_weight,
    query_bias,
    value_bias,
    proj_weight,
    proj_bias,
    attn_scale,
    norm2_gain,
    norm2_bias,
    inner_weight,
    inner_bias,
    outer_weight,
    outer_bias,
    mlp_scale,
):
    first = lax.axis_index("section") == 0
    y = lax.axis_index("row")

    small = (query_bias, value_bias, inner_bias)
    vectors = (norm1_gain, norm1_bias, proj_bias, attn_scale, norm2_gain, norm2_bias, outer_bias, mlp_scale)
    vectors = (jnp.concatenate(vectors, axis=0),)
    kept, sent = cut_weights(first, qkv_weight[0], proj_weight[0], inner_weight[0], outer_weight[0], *small, *vectors)
    got = swap_core(sent)
    vec_got, got = got[272:, :256], got[:272]
    blocks0, blocks1 = jnp.where(first, kept[:272], got), jnp.where(first, got, kept[:272])
    vec = kept[272:, :256]
    vecs = jnp.concatenate([jnp.where(first, vec, vec_got), jnp.where(first, vec_got, vec)], axis=0)

    tiles = tiles_gathered(jnp.concatenate([blocks0[:, 128:], blocks1], axis=1))

    paired = jnp.stack([block_input, cotangent]).reshape(2, 4, 2, 64, 256)
    paired = jnp.where(first, paired[:, :, 0], paired[:, :, 1])
    shared = jnp.concatenate([vecs, jnp.concatenate([blocks0[:128, :128], blocks0[128:256, :128]], axis=1)], axis=0)
    messages = []
    for k in (0, 3, 1, 2):
        chunk = lax.dynamic_index_in_dim(paired, (y + k) % 4, 1, keepdims=False).reshape(128, 256)
        messages.append(jnp.concatenate([chunk, shared], axis=0))
    got = scatter4(messages, "row")
    ordered = jnp.stack([got[0], got[1], got[3], got[2]])
    ordered = lax.dynamic_slice_in_dim(jnp.concatenate([ordered, ordered]), (4 - y) % 4, 4, 0)
    tokens = jnp.concatenate([ordered[i, :128] for i in range(4)], axis=1).astype(f32)
    vecs = jnp.concatenate([ordered[i, 128:160] for i in range(4)], axis=1).astype(f32)
    att = jnp.concatenate([ordered[:, 160:, :128], ordered[:, 160:, 128:]], axis=1).reshape(1024, 128)
    att = jnp.concatenate([att, blocks0[256:264, :128]], axis=0)
    att = jnp.concatenate(gather4(att, "x"), axis=1)

    tiles_att1 = [t[:, :, 256:384] for t in tiles]
    att1 = jnp.concatenate([rows_of(tiles_att1, 256), jnp.concatenate([t[0, 256:264] for t in tiles_att1], axis=1)])
    w0 = {"vec": vecs[0:8] + vecs[8:16], "att": att, "first": first, **ffn_weights(tiles, 0)}
    w1 = {"vec": vecs[16:24] + vecs[24:32], **att_weights(att1, first), **ffn_weights(tiles, 384)}

    used = jnp.where(y < 2, images_used[0], images_used[1])
    live = (lax.axis_index("x") < used).astype(f32)

    seed = live * tokens[64:]
    vec0, vec1 = w0["vec"], w1["vec"]
    seed_low = (seed * vec1[7]).astype(bf16)
    hidden0, contracted0, norm0, one0, two0, gcs1 = forward(tokens[:64], w0, seed_low)
    seed_low, gcs1 = gcs1
    handed = (hidden0 + vec0[7] * contracted0).astype(bf16).astype(f32)
    hidden1, contracted1, norm1, one1, two1, _ = forward(handed, w1, None, True)


    grad_hidden1, grad_second1, ga1, ffn1 = backward_ffn(seed, seed_low, gcs1, two1, w1)
    gas1 = gather_tokens(ga1)
    dq1, near1, pair1 = backward_att(gas1, one1, w1)
    contracted1, pair1 = lax.optimization_barrier((contracted1(pair1), swap_pair(pair1)))
    dkv1 = (near1 + pair1.astype(f32)).astype(bf16)
    partial1 = dot_t(dkv1, w1["kv"]) + dot_t(dq1, w1["qp"])
    final = (live * (hidden1 + vec1[7] * contracted1)).astype(bf16)
    grad_normed1 = scatter_tokens(partial1)
    att1 = att_operands(first, dkv1, dq1, gas1, one1)
    blocks1 = sum_over(block_grads(layer_grads_kernel, 416, ffn1 + att1), "x")
    rows1 = row_sums(
        True, grad_normed1, norm1[0], vec1, ga1, grad_hidden1, norm1[2], grad_second1, two1[0], seed_low, seed, contracted1
    )
    back1 = grad_hidden1 + norm_back(grad_normed1, norm1[0], norm1[1], vec1[0])
    g0 = back1.astype(bf16).astype(f32)

    gc0 = (g0 * vec0[7]).astype(bf16)
    gcs0 = gather_tokens(gc0)
    grad_hidden0, grad_second0, ga0, ffn0 = backward_ffn(g0, gc0, gcs0, two0, w0)
    parts = gather4(jnp.concatenate([ga0, rows1.astype(bf16)], axis=0), "z")
    parts, blocks1 = lax.optimization_barrier((parts, blocks1))
    gas0, rows1 = jnp.concatenate([p[:64] for p in parts], axis=0), sum4([p[64:] for p in parts])
    dq0, near0, pair0 = backward_att(gas0, one0, w0)
    mixed = sum_over(block_grads(ffn_grads_kernel, 272, ffn0), "x")
    mixed = sum_over(jnp.concatenate([mixed, blocks1], axis=1), "row")
    dkv0 = (near0 + swap_pair(pair0).astype(f32)).astype(bf16)
    partial0 = dot_t(dkv0, w0["kv"]) + dot_t(dq0, w0["qp"])
    att0 = att_operands(first, dkv0, dq0, gas0, one0)
    rows0 = row_sums(
        False, partial0, one0[0], vec0, ga0, grad_hidden0, norm0[2], grad_second0, two0[0], gc0, g0, contracted0
    )
    att0 = block_grads(att_grads_kernel, 144, att0)
    low, att0 = lax.optimization_barrier((partial0.astype(bf16), att0))
    rows0 = rows0.astype(bf16)
    parts = scatter4([jnp.concatenate([low[i * 64 : (i + 1) * 64], rows0], axis=0) for i in range(4)], "z")
    att0 = reduce_x(att0)
    grad_normed0, rows0 = sum4([p[:64] for p in parts]), sum4([p[64:] for p in parts])
    rows = sum4(gather4(jnp.concatenate([rows0, rows1], axis=0).astype(bf16), "x")).astype(bf16)
    grad_in = (grad_hidden0 + norm_back(grad_normed0, norm0[0], norm0[1], vec0[0])).astype(bf16)

    own = jnp.where(first, grad_in, final)
    got = swap_core(jnp.where(first, final, grad_in))
    edge = jnp.concatenate([jnp.where(first, own, got), jnp.where(first, got, own), rows], axis=0)
    edge = jnp.stack([edge[:, i * 256 : (i + 1) * 256] for i in range(4)])
    got = scatter4(to_slots(jnp.concatenate([edge, att0], axis=1)), "row")
    got, mixed = lax.optimization_barrier((got, mixed))
    edge = in_order([p[:128] for p in got]).reshape(1, 2, 256, 256).astype(f32)
    rest = sum4([p[128:] for p in got]).astype(bf16)

    layer0 = jnp.concatenate([mixed[:272], rest[16:], rest[:8]], axis=0)
    layer1 = jnp.concatenate([mixed[272:], rest[8:16]], axis=0)
    far = swap_core(jnp.where(first, layer1, layer0))
    qkv, qb, vb, proj, inner, ib, outer, rows = assemble(first, jnp.where(first, layer0, layer1), far)

    return (
        edge,
        rows[0][None],
        rows[1][None],
        qkv[None],
        qb,
        vb,
        proj[None],
        rows[2][None],
        rows[3][None],
        rows[4][None],
        rows[5][None],
        inner[None],
        ib,
        outer[None],
        rows[6][None],
        rows[7][None],
    )


def solution(mesh):
    grid = Mesh(mesh.devices.reshape(2, 4, 4, 4), ("section", "row", "x", "z"))
    col = ("x", "z")
    by_row = P("section", "row")
    by_col = P("section", col)
    matrix = P("section", "row", col)
    matrix_t = P("section", col, "row")
    return jax.shard_map(
        local,
        mesh=grid,
        in_specs=(
            P(None, col, "row"),
            P(None, col, "row"),
            P(),
            by_row,
            by_row,
            matrix,
            by_col,
            by_col,
            matrix_t,
            by_row,
            by_row,
            by_row,
            by_row,
            matrix,
            by_col,
            matrix_t,
            by_row,
            by_row,
        ),
        out_specs=(
            P("section", None, col, "row"),
            by_row,
            by_row,
            matrix,
            by_col,
            by_col,
            matrix_t,
            by_row,
            by_row,
            by_row,
            by_row,
            matrix,
            by_col,
            matrix_t,
            by_row,
            by_row,
        ),
        check_vma=False,
    )
```

```python
import functools

import jax
import jax.numpy as jnp
from jax import lax
from jax.experimental import pallas as pl
from jax.experimental.pallas import tpu as pltpu
from jax.sharding import Mesh
from jax.sharding import PartitionSpec as P

HD = 64
norm_eps = 1e-06
bf16 = jnp.bfloat16
f32 = jnp.float32
SCALE = HD ** (-0.5)


def shift(v, axis, by):
    return lax.ppermute(v, axis, [(i, (i + by) % 4) for i in range(4)])


def gather4(v, axis):
    far = shift(v, axis, 2)
    return [v, shift(v, axis, 1), shift(v, axis, 3), far]


def scatter4(parts, axis):
    far = shift(parts[3], axis, 2)
    return [parts[0], shift(parts[1], axis, 3), shift(parts[2], axis, 1), far]


def sum4(parts):
    a, b, c, d = [p.astype(f32) for p in parts]
    return (a + b) + (c + d)


def swap_core(v):
    return lax.ppermute(v, "section", [(0, 1), (1, 0)])


def swap_pair(v):
    return lax.ppermute(v, "row", [(0, 1), (1, 0), (2, 3), (3, 2)])


def gather_tokens(rows):
    return jnp.concatenate(gather4(rows, "z"), axis=0)


def scatter_tokens(partial):
    low = partial.astype(bf16)
    n = low.shape[0] // 4
    return sum4(scatter4([low[i * n : (i + 1) * n] for i in range(4)], "z"))


def dot(a, b):
    return jnp.dot(a, b, preferred_element_type=f32)


def dot_t(a, b):
    return lax.dot_general(a, b, (((1,), (1,)), ((), ())), preferred_element_type=f32)


def t_dot(a, b):
    return lax.dot_general(a, b, (((0,), (0,)), ((), ())), preferred_element_type=f32)


def norm_local(features, gain, bias):
    center = jnp.mean(features, axis=-1, keepdims=True)
    offset = features - center
    spread = jnp.mean(offset * offset, axis=-1, keepdims=True)
    inverse = lax.rsqrt(spread + norm_eps)
    scaled = offset * inverse
    return scaled * gain + bias, scaled, inverse


def norm_back(upstream, scaled, inverse, gain):
    weighted = upstream * gain
    first = jnp.mean(weighted, axis=-1, keepdims=True)
    second = jnp.mean(weighted * scaled, axis=-1, keepdims=True)
    return inverse * (weighted - first - scaled * second)


def gelu_both(v):
    cdf = 0.5 * (1.0 + lax.erf(v * (0.5**0.5)))
    density = jnp.exp(-0.5 * v * v) * 0.3989422804014327
    return (v * cdf).astype(bf16), cdf + v * density


def attend_kernel(q_ref, own_ref, core_ref, pair_ref, both_ref, o_ref, lt_ref):
    q = q_ref[...]
    kv = jnp.concatenate([own_ref[...], core_ref[...], pair_ref[...], both_ref[...]], axis=0)
    s = dot_t(q, kv) * SCALE
    peak = jnp.max(s, axis=-1, keepdims=True)
    raised = jnp.exp(s - peak)
    total = jnp.sum(raised, axis=-1, keepdims=True)
    low = (raised * (1.0 / total)).astype(bf16)
    o = dot(low, kv)
    upper = lax.broadcasted_iota(jnp.int32, o.shape, 1) >= HD
    o_ref[...] = jnp.where(upper, o, 0.0).astype(bf16)
    lt_ref[...] = jnp.broadcast_to(peak + jnp.log(total), lt_ref.shape)


def attend(q, kvs):
    tokens, width = q.shape
    spec = pl.BlockSpec((tokens, 128), lambda h: (0, h))
    return pl.pallas_call(
        attend_kernel,
        grid=(width // 128,),
        in_specs=[spec] * 5,
        out_specs=[spec, spec],
        out_shape=[
            jax.ShapeDtypeStruct((tokens, width), bf16),
            jax.ShapeDtypeStruct((tokens, width), f32),
        ],
        compiler_params=pltpu.CompilerParams(vmem_limit_bytes=32 * 2**20),
        cost_estimate=pl.CostEstimate(flops=4 * 2 * 2 * 256 * 1024 * 128, bytes_accessed=2**21, transcendentals=2**20),
    )(q, *kvs)


def attend_back_kernel(
    q_ref, own_ref, core_ref, pair_ref, both_ref, g_ref, lt_ref, dq_ref, down_ref, dcore_ref, dpair_ref, dboth_ref
):
    q = q_ref[...]
    n = q.shape[0]
    upper = lax.broadcasted_iota(jnp.int32, q.shape, 1) >= HD
    g = jnp.where(upper, g_ref[...], jnp.zeros_like(q))
    kv = jnp.concatenate([own_ref[...], core_ref[...], pair_ref[...], both_ref[...]], axis=0)
    s = dot_t(q, kv) * SCALE
    probs = jnp.exp(s - lt_ref[:, 0:1])
    grad_probs = dot_t(g, kv)
    along = jnp.sum(probs * grad_probs, axis=-1, keepdims=True)
    ds = (probs * (grad_probs - along)).astype(bf16)
    low = probs.astype(bf16)
    dq = dot(ds, kv) * SCALE
    dq_ref[...] = jnp.where(upper, 0.0, dq).astype(bf16)
    dkv = t_dot(ds, q) * SCALE + t_dot(low, g)
    down_ref[...] = dkv[0:n].astype(down_ref.dtype)
    dcore_ref[...] = dkv[n : 2 * n].astype(dcore_ref.dtype)
    dpair_ref[...] = dkv[2 * n : 3 * n].astype(dpair_ref.dtype)
    dboth_ref[...] = dkv[3 * n :].astype(dboth_ref.dtype)


def attend_back(q, kvs, g, lt):
    tokens, width = q.shape
    spec = pl.BlockSpec((tokens, 128), lambda h: (0, h))
    return pl.pallas_call(
        attend_back_kernel,
        grid=(width // 128,),
        in_specs=[spec] * 7,
        out_specs=[spec] * 5,
        out_shape=[
            jax.ShapeDtypeStruct((tokens, width), bf16),
            jax.ShapeDtypeStruct((tokens, width), f32),
            jax.ShapeDtypeStruct((tokens, width), bf16),
            jax.ShapeDtypeStruct((tokens, width), f32),
            jax.ShapeDtypeStruct((tokens, width), bf16),
        ],
        compiler_params=pltpu.CompilerParams(vmem_limit_bytes=40 * 2**20),
        cost_estimate=pl.CostEstimate(flops=4 * 5 * 2 * 256 * 1024 * 128, bytes_accessed=2**22, transcendentals=2**20),
    )(q, *kvs, g, lt)


def tile_of(out_ref, i):
    return out_ref[i] if isinstance(out_ref, tuple) else out_ref.at[i]


def store_sums(out_ref, at, a, b):
    sums = jnp.sum(a[...].astype(f32), axis=0, keepdims=True) + jnp.sum(b[...].astype(f32), axis=0, keepdims=True)
    for i in range(4):
        row = jnp.concatenate([sums[:, i * 128 : (i + 1) * 128], jnp.zeros((1, 128), f32)], axis=1)
        tile_of(out_ref, i)[0, at : at + 16, :] = jnp.broadcast_to(row, (16, 256)).astype(bf16)


def store_tiles(out_ref, at, d):
    for i in range(4):
        tile_of(out_ref, i)[0, at : at + 128, :] = d[i * 128 : (i + 1) * 128].astype(bf16)


def ffn_part(out_ref, at, ge, ge_far, act, act_far, x, x_far, g, g_far):
    store_tiles(out_ref, at, t_dot(ge[...], x[...]) + t_dot(ge_far[...], x_far[...]))
    store_tiles(out_ref, at + 128, t_dot(act[...], g[...]) + t_dot(act_far[...], g_far[...]))
    store_sums(out_ref, at + 256, ge, ge_far)


def att_part(out_ref, at, m, m_far, o, o_far, x, x_far, g, g_far, mask_ref):
    d_proj = t_dot(o[...], g[...]) + t_dot(o_far[...], g_far[...])
    store_tiles(out_ref, at, t_dot(m[...], x[...]) + t_dot(m_far[...], x_far[...]) + mask_ref[...] * d_proj)
    store_sums(out_ref, at + 128, m, m_far)


def ffn_grads_kernel(*refs):
    ffn_part(refs[-1], 0, *refs[:8])


def att_grads_kernel(*refs):
    att_part(refs[-4:], 0, *refs[:9])


def layer_grads_kernel(*refs):
    ffn_part(refs[-1], 0, *refs[:8])
    att_part(refs[-1], 272, *refs[8:17])


def block_grads(kernel, rows, operands, apart=False):
    specs = []
    for v in operands:
        if v.shape[1] == 1024:
            specs.append(pl.BlockSpec((v.shape[0], 256), lambda j: (0, j)))
        else:
            specs.append(pl.BlockSpec(v.shape, lambda j: (0, 0)))
    return pl.pallas_call(
        kernel,
        grid=(4,),
        in_specs=specs,
        out_specs=[pl.BlockSpec((1, rows, 256), lambda j: (j, 0, 0))] * 4
        if apart
        else pl.BlockSpec((4, 1, rows, 256), lambda j: (0, j, 0, 0)),
        out_shape=[jax.ShapeDtypeStruct((4, rows, 256), bf16)] * 4
        if apart
        else jax.ShapeDtypeStruct((4, 4, rows, 256), bf16),
        compiler_params=pltpu.CompilerParams(vmem_limit_bytes=60 * 2**20),
        cost_estimate=pl.CostEstimate(flops=rows * 2**24, bytes_accessed=8 * 2**20, transcendentals=0),
    )(*operands)


def assemble_kernel(first_ref, mine_ref, got_ref, qkv, qb, vb, proj, inner, ib, outer, rows):
    mine, got = mine_ref[...].astype(f32), got_ref[...].astype(f32)
    first = first_ref[0] == 0
    h0, h1 = jnp.where(first, mine, got), jnp.where(first, got, mine)
    inner[...] = jnp.concatenate([h0[0:128], h1[0:128]], axis=0).T
    outer[...] = jnp.concatenate([h0[128:256], h1[128:256]], axis=0)
    ib[...] = jnp.concatenate([h0[256:257, :128], h1[256:257, :128]], axis=1)
    qkv[...] = jnp.concatenate([h1[272:336], h0[272:400]], axis=0)
    proj[...] = h1[336:400]
    qb[...] = h1[400:401, :HD]
    vb[...] = h0[400:401, HD:128]
    rows[...] = h0[416:424] + h1[416:424]


def assemble(first, mine, got):
    shapes = [(192, 256), (1, HD), (1, HD), (64, 256), (256, 256), (1, 256), (256, 256), (8, 256)]
    vmem = pl.BlockSpec(memory_space=pltpu.VMEM)
    return pl.pallas_call(
        assemble_kernel,
        in_specs=[pl.BlockSpec(memory_space=pltpu.SMEM), vmem, vmem],
        out_shape=[jax.ShapeDtypeStruct(v, f32) for v in shapes],
        compiler_params=pltpu.CompilerParams(vmem_limit_bytes=32 * 2**20),
    )(jnp.where(first, 0, 1).astype(jnp.int32).reshape(1), mine, got)


def rows_kernel(direct, a, b, vec, ga, gh, att, gs, n2, gc, g, con, *rest):
    out_ref = rest[-1]
    left = a[...]
    right = b[...] if direct else (b[...].astype(f32) - vec[1:2, :]) * (1.0 / vec[0:1, :])
    out_ref[0:1, :] = jnp.sum(left * right, axis=0, keepdims=True)
    out_ref[1:2, :] = jnp.sum(left, axis=0, keepdims=True)
    out_ref[2:3, :] = jnp.sum(ga[...].astype(f32), axis=0, keepdims=True)
    out_ref[3:4, :] = jnp.sum(gh[...] * att[...], axis=0, keepdims=True)
    out_ref[4:5, :] = jnp.sum(gs[...] * n2[...], axis=0, keepdims=True)
    out_ref[5:6, :] = jnp.sum(gs[...], axis=0, keepdims=True)
    out_ref[6:7, :] = jnp.sum(gc[...].astype(f32), axis=0, keepdims=True)
    if direct:
        total = jnp.sum(rest[0][...].astype(f32) * con[...].astype(f32), axis=0, keepdims=True)
        total = total * (1.0 / vec[7:8, :]) + vec[6:7, :] * jnp.sum(g[...], axis=0, keepdims=True)
        out_ref[7:8, :] = total
    else:
        out_ref[7:8, :] = jnp.sum(g[...] * con[...], axis=0, keepdims=True)


def row_sums(direct, *arrays):
    return pl.pallas_call(
        functools.partial(rows_kernel, direct),
        out_shape=jax.ShapeDtypeStruct((8, 1024), f32),
        compiler_params=pltpu.CompilerParams(vmem_limit_bytes=32 * 2**20),
        cost_estimate=pl.CostEstimate(flops=2**21, bytes_accessed=4 * 2**20, transcendentals=0),
    )(*arrays)


def forward(u, w, beside=None, late=False):
    vec = w["vec"]
    lower = (jnp.arange(512) % 128) < HD
    n1, scaled1, inv1 = norm_local(u, vec[0], vec[1])
    x = gather_tokens(n1.astype(bf16))
    if "att" in w:
        att, x = lax.optimization_barrier((w["att"], x))
        w.update(att_weights(att, w["first"]))
    kv = (dot(x, w["kv"]) + w["kv_bias"]).astype(bf16)
    if beside is not None:
        kv, beside = lax.optimization_barrier((kv, beside))
    kv_pair = swap_pair(kv)
    q = (jnp.where(lower, dot(x, w["qp"]), 0.0) + w["q_bias"]).astype(bf16)
    if beside is not None:
        kv_pair, beside = lax.optimization_barrier((kv_pair, (beside, gather_tokens(beside))))
    kvs = (kv, swap_core(kv), kv_pair, swap_core(kv_pair))
    o, lt = attend(q, kvs)
    attended = scatter_tokens(dot_t(o, w["qp"])) + vec[2]
    hidden = u + vec[3] * attended
    n2, scaled2, inv2 = norm_local(hidden, vec[4], vec[5])
    x2 = gather_tokens(n2.astype(bf16))
    a_own, da_own = gelu_both(dot(x2, w["in_own"]) + w["in_bias_own"])
    a_oth, da_oth = gelu_both(dot(x2, w["in_oth"]) + w["in_bias_oth"])
    partial = (dot_t(a_own, w["out_own"]) + dot_t(a_oth, w["out_oth"])).astype(bf16)
    contracted = partial if late else scatter_tokens(partial) + vec[6]
    one, two = (x, kvs, q, o, lt), (scaled2, inv2, x2, a_own, da_own, a_oth, da_oth)
    return hidden, contracted, (scaled1, inv1, attended), one, two, beside


def reduce_x(blocks):
    return sum4(scatter4(blocks, "x")).astype(bf16)


def reduce_y(blocks):
    return sum4(scatter4(to_slots(blocks), "row")).astype(bf16)


def to_slots(blocks):
    y = lax.axis_index("row")
    return [lax.dynamic_index_in_dim(blocks, (y + k) % 4, 0, keepdims=False) for k in (0, 3, 1, 2)]


def in_order(parts):
    y = lax.axis_index("row")
    stacked = jnp.stack([parts[0], parts[1], parts[3], parts[2]])
    return lax.dynamic_slice_in_dim(jnp.concatenate([stacked, stacked]), (4 - y) % 4, 4, 0)


def backward_ffn(g, gc, gcs, saved, w):
    scaled2, inv2, x2, a_own, da_own, a_oth, da_oth = saved
    ge_own = (dot(gcs, w["out_own"]) * da_own).astype(bf16)
    ge_oth = (dot(gcs, w["out_oth"]) * da_oth).astype(bf16)
    grad_second = scatter_tokens(dot_t(ge_own, w["in_own"]) + dot_t(ge_oth, w["in_oth"]))
    grad_hidden = g + norm_back(grad_second, scaled2, inv2, w["vec"][4])
    ga = (grad_hidden * w["vec"][3]).astype(bf16)
    operands = (ge_own, swap_core(ge_oth), a_own, swap_core(a_oth), x2, swap_core(x2), gcs, swap_core(gcs))
    return grad_hidden, grad_second, ga, operands


def backward_att(gas, saved, w):
    x, kvs, q, o, lt = saved
    gz = dot(gas, w["qp"]).astype(bf16)
    dq, d_own, d_core, d_pair, d_both = attend_back(q, kvs, gz, lt)
    pair_sum = (d_pair + swap_core(d_both).astype(f32)).astype(bf16)
    near = d_own + swap_core(d_core).astype(f32)
    return dq, near, pair_sum


def att_operands(first, dkv, dq, gas, saved):
    x, _, _, o, _ = saved
    return (
        jnp.where(first, dkv, dq),
        swap_core(jnp.where(first, dq, dkv)),
        o,
        swap_core(o),
        x,
        swap_core(x),
        gas,
        swap_core(gas),
        jnp.full((1, 256), jnp.where(first, 0.0, 1.0), f32),
    )


def rows_of(tiles, n):
    return jnp.concatenate([t[:, :n].reshape(-1, t.shape[2]) for t in tiles], axis=1)


def tiles_gathered(half):
    tiles = lax.all_gather(half, ("x", "row"), axis=0, tiled=True).reshape(4, 4, *half.shape)
    return [tiles[i] for i in range(4)]


def split(v):
    high = v.astype(bf16).astype(f32)
    return high, v - high


def cut_weights_kernel(first_ref, qkv_ref, proj_ref, inner_ref, outer_ref, qb, vb, ib, *refs):
    vectors, kept_ref, sent_ref = refs[:8], refs[8], refs[9]
    mine = first_ref[0] == 0
    qkv = qkv_ref[...].astype(f32).T
    outer_t = outer_ref[...].astype(f32).T
    inner = inner_ref[...].astype(f32)
    kv = qkv[:, HD:]
    qp = jnp.concatenate([qkv[:, :HD], proj_ref[...].astype(f32).T], axis=1)
    none = jnp.zeros((1, HD), f32)
    bias0 = jnp.concatenate([none, vb[...], ib[:, :128], none, none], axis=1)
    bias1 = jnp.concatenate([qb[...], none, ib[:, 128:], none, none], axis=1)
    pad = jnp.zeros((14, 384), f32)
    half0 = [jnp.concatenate([kv, inner[:, :128], outer_t[:, :128]], axis=1), *split(bias0), pad]
    half1 = [jnp.concatenate([qp, inner[:, 128:], outer_t[:, 128:]], axis=1), *split(bias1), pad]
    vec = jnp.concatenate(split(jnp.concatenate([v[...] for v in vectors], axis=0)), axis=0)
    vec = jnp.concatenate([vec, jnp.zeros((16, 128), f32)], axis=1)
    half0 = jnp.concatenate([*half0, vec], axis=0)
    half1 = jnp.concatenate([*half1, vec], axis=0)
    kept_ref[...] = jnp.where(mine, half0, half1).astype(bf16)
    sent_ref[...] = jnp.where(mine, half1, half0).astype(bf16)


def cut_weights(first, *arrays):
    place = pl.BlockSpec(memory_space=pltpu.SMEM)
    return pl.pallas_call(
        cut_weights_kernel,
        in_specs=[place] + [pl.BlockSpec(memory_space=pltpu.VMEM)] * len(arrays),
        out_shape=[jax.ShapeDtypeStruct((288, 384), bf16)] * 2,
        compiler_params=pltpu.CompilerParams(vmem_limit_bytes=60 * 2**20),
    )(jnp.where(first, 0, 1).astype(jnp.int32).reshape(1), *arrays)


def joined(rows):
    return rows[0].astype(f32) + rows[1].astype(f32)


def att_weights(att, first):
    far = swap_core(att)
    kv, qp = jnp.where(first, att, far), jnp.where(first, far, att)
    return {"kv": kv[:1024], "qp": qp[:1024], "kv_bias": joined(kv[1024:]), "q_bias": joined(qp[1024:])}


def ffn_weights(tiles, at):
    in_own = rows_of([t[:, :, at : at + 128] for t in tiles], 256)
    out_own = rows_of([t[:, :, at + 128 : at + 256] for t in tiles], 256)
    bias = jnp.concatenate([joined(t[0, 256:258, at : at + 128]) for t in tiles])
    return {
        "in_own": in_own,
        "out_own": out_own,
        "in_oth": swap_core(in_own),
        "out_oth": swap_core(out_own),
        "in_bias_own": bias,
        "in_bias_oth": swap_core(bias),
    }


def sum_over(blocks, axis):
    rows = blocks.reshape(-1, blocks.shape[-1])
    return lax.psum_scatter(rows, axis, scatter_dimension=0, tiled=True).reshape(blocks.shape[1:])


def local(
    block_input,
    cotangent,
    images_used,
    norm1_gain,
    norm1_bias,
    qkv_weight,
    query_bias,
    value_bias,
    proj_weight,
    proj_bias,
    attn_scale,
    norm2_gain,
    norm2_bias,
    inner_weight,
    inner_bias,
    outer_weight,
    outer_bias,
    mlp_scale,
):
    first = lax.axis_index("section") == 0
    y = lax.axis_index("row")

    small = (query_bias, value_bias, inner_bias)
    vectors = (norm1_gain, norm1_bias, proj_bias, attn_scale, norm2_gain, norm2_bias, outer_bias, mlp_scale)
    kept, sent = cut_weights(first, qkv_weight[0].T, proj_weight[0], inner_weight[0], outer_weight[0], *small, *vectors)
    got = swap_core(sent)
    vec_got, got = got[272:, :256], got[:272]
    blocks0, blocks1 = jnp.where(first, kept[:272], got), jnp.where(first, got, kept[:272])
    vec = kept[272:, :256]
    vecs = jnp.concatenate([jnp.where(first, vec, vec_got), jnp.where(first, vec_got, vec)], axis=0)

    tiles = tiles_gathered(jnp.concatenate([blocks0[:, 128:], blocks1], axis=1))

    paired = jnp.stack([block_input, cotangent]).reshape(2, 4, 2, 64, 256)
    paired = jnp.where(first, paired[:, :, 0], paired[:, :, 1])
    shared = jnp.concatenate([vecs, jnp.concatenate([blocks0[:128, :128], blocks0[128:256, :128]], axis=1)], axis=0)
    messages = []
    for k in (0, 3, 1, 2):
        chunk = lax.dynamic_index_in_dim(paired, (y + k) % 4, 1, keepdims=False).reshape(128, 256)
        messages.append(jnp.concatenate([chunk, shared], axis=0))
    got = scatter4(messages, "row")
    ordered = jnp.stack([got[0], got[1], got[3], got[2]])
    ordered = lax.dynamic_slice_in_dim(jnp.concatenate([ordered, ordered]), (4 - y) % 4, 4, 0)
    tokens = jnp.concatenate([ordered[i, :128] for i in range(4)], axis=1).astype(f32)
    vecs = jnp.concatenate([ordered[i, 128:160] for i in range(4)], axis=1).astype(f32)
    att = jnp.concatenate([ordered[:, 160:, :128], ordered[:, 160:, 128:]], axis=1).reshape(1024, 128)
    att = jnp.concatenate([att, blocks0[256:264, :128]], axis=0)
    att = jnp.concatenate(gather4(att, "x"), axis=1)

    tiles_att1 = [t[:, :, 256:384] for t in tiles]
    att1 = jnp.concatenate([rows_of(tiles_att1, 256), jnp.concatenate([t[0, 256:264] for t in tiles_att1], axis=1)])
    w0 = {"vec": vecs[0:8] + vecs[8:16], "att": att, "first": first, **ffn_weights(tiles, 0)}
    w1 = {"vec": vecs[16:24] + vecs[24:32], **att_weights(att1, first), **ffn_weights(tiles, 384)}

    used = jnp.where(y < 2, images_used[0], images_used[1])
    live = (lax.axis_index("x") < used).astype(f32)

    seed = live * tokens[64:]
    vec0, vec1 = w0["vec"], w1["vec"]
    seed_low = (seed * vec1[7]).astype(bf16)
    hidden0, contracted0, norm0, one0, two0, gcs1 = forward(tokens[:64], w0, seed_low)
    seed_low, gcs1 = gcs1
    handed = (hidden0 + vec0[7] * contracted0).astype(bf16).astype(f32)
    hidden1, contracted1, norm1, one1, two1, _ = forward(handed, w1, None, True)


    grad_hidden1, grad_second1, ga1, ffn1 = backward_ffn(seed, seed_low, gcs1, two1, w1)
    gas1 = gather_tokens(ga1)
    dq1, near1, pair1 = backward_att(gas1, one1, w1)
    dkv1 = (near1 + swap_pair(pair1).astype(f32)).astype(bf16)
    partial1 = dot_t(dkv1, w1["kv"]) + dot_t(dq1, w1["qp"])
    grad_normed1 = scatter_tokens(partial1)
    att1 = att_operands(first, dkv1, dq1, gas1, one1)
    blocks1 = sum_over(block_grads(ffn_grads_kernel, 272, ffn1), "x")
    back1 = grad_hidden1 + norm_back(grad_normed1, norm1[0], norm1[1], vec1[0])
    g0 = back1.astype(bf16).astype(f32)

    gc0 = (g0 * vec0[7]).astype(bf16)
    gcs0 = gather_tokens(gc0)
    grad_hidden0, grad_second0, ga0, ffn0 = backward_ffn(g0, gc0, gcs0, two0, w0)
    gas0 = gather_tokens(ga0)
    dq0, near0, pair0 = backward_att(gas0, one0, w0)
    mixed = sum_over(block_grads(layer_grads_kernel, 416, ffn0 + att1), "x")
    dkv0 = (near0 + swap_pair(pair0).astype(f32)).astype(bf16)
    partial0 = dot_t(dkv0, w0["kv"]) + dot_t(dq0, w0["qp"])
    partial0, mixed = lax.optimization_barrier((partial0, mixed))
    mixed, blocks1 = sum_over(mixed, "row"), sum_over(blocks1, "row")
    rows1 = row_sums(
        True, grad_normed1, norm1[0], vec1, ga1, grad_hidden1, norm1[2], grad_second1, two1[0], seed_low, seed, contracted1, gcs1
    )
    att0 = att_operands(first, dkv0, dq0, gas0, one0)
    rows0 = row_sums(
        False, partial0, one0[0], vec0, ga0, grad_hidden0, norm0[2], grad_second0, two0[0], gc0, g0, contracted0
    )
    att0 = block_grads(att_grads_kernel, 144, att0, True)
    low, att0 = lax.optimization_barrier((partial0.astype(bf16), att0))
    rows0 = jnp.concatenate([rows0, rows1], axis=0).astype(bf16)
    cuts = [slice(i * 64, (i + 1) * 64) for i in range(4)]
    parts = scatter4([jnp.concatenate([low[c], rows0, contracted1[c]], axis=0) for c in cuts], "z")
    contracted1 = sum4([p[80:] for p in parts]) + vec1[6]
    final = (live * (hidden1 + vec1[7] * contracted1)).astype(bf16)
    att0 = reduce_x(att0)
    grad_normed0, rows0 = sum4([p[:64] for p in parts]), sum4([p[64:80] for p in parts])
    rows = sum4(gather4(rows0.astype(bf16), "x")).astype(bf16)
    grad_in = (grad_hidden0 + norm_back(grad_normed0, norm0[0], norm0[1], vec0[0])).astype(bf16)

    own = jnp.where(first, grad_in, final)
    got = swap_core(jnp.where(first, final, grad_in))
    edge = jnp.concatenate([jnp.where(first, own, got), jnp.where(first, got, own), rows], axis=0)
    edge = jnp.stack([edge[:, i * 256 : (i + 1) * 256] for i in range(4)])
    got = scatter4(to_slots(jnp.concatenate([edge, att0], axis=1)), "row")
    got, mixed, blocks1 = lax.optimization_barrier((got, mixed, blocks1))
    edge = in_order([p[:128] for p in got]).reshape(1, 2, 256, 256).astype(f32)
    rest = sum4([p[128:] for p in got]).astype(bf16)

    layer0 = jnp.concatenate([mixed[:272], rest[16:], rest[:8]], axis=0)
    layer1 = jnp.concatenate([blocks1, mixed[272:], rest[8:16]], axis=0)
    far = swap_core(jnp.where(first, layer1, layer0))
    qkv, qb, vb, proj, inner, ib, outer, rows = assemble(first, jnp.where(first, layer0, layer1), far)

    return (
        edge,
        rows[0][None],
        rows[1][None],
        qkv.T[None],
        qb,
        vb,
        proj[None],
        rows[2][None],
        rows[3][None],
        rows[4][None],
        rows[5][None],
        inner[None],
        ib,
        outer[None],
        rows[6][None],
        rows[7][None],
    )


def solution(mesh):
    grid = Mesh(mesh.devices.reshape(2, 4, 4, 4), ("section", "row", "x", "z"))
    col = ("x", "z")
    by_row = P("section", "row")
    by_col = P("section", col)
    matrix = P("section", "row", col)
    matrix_t = P("section", col, "row")
    return jax.shard_map(
        local,
        mesh=grid,
        in_specs=(
            P(None, col, "row"),
            P(None, col, "row"),
            P(),
            by_row,
            by_row,
            matrix,
            by_col,
            by_col,
            matrix_t,
            by_row,
            by_row,
            by_row,
            by_row,
            matrix,
            by_col,
            matrix_t,
            by_row,
            by_row,
        ),
        out_specs=(
            P("section", None, col, "row"),
            by_row,
            by_row,
            matrix,
            by_col,
            by_col,
            matrix_t,
            by_row,
            by_row,
            by_row,
            by_row,
            matrix,
            by_col,
            matrix_t,
            by_row,
            by_row,
        ),
        check_vma=False,
    )
```

```python
import functools

import jax
import jax.numpy as jnp
from jax import lax
from jax.experimental import pallas as pl
from jax.experimental.pallas import tpu as pltpu
from jax.sharding import Mesh
from jax.sharding import PartitionSpec as P

HD = 64
norm_eps = 1e-06
bf16 = jnp.bfloat16
f32 = jnp.float32
SCALE = HD ** (-0.5)


def shift(v, axis, by):
    return lax.ppermute(v, axis, [(i, (i + by) % 4) for i in range(4)])


def gather4(v, axis):
    far = shift(v, axis, 2)
    return [v, shift(v, axis, 1), shift(v, axis, 3), far]


def scatter4(parts, axis):
    far = shift(parts[3], axis, 2)
    return [parts[0], shift(parts[1], axis, 3), shift(parts[2], axis, 1), far]


def sum4(parts):
    a, b, c, d = [p.astype(f32) for p in parts]
    return (a + b) + (c + d)


def swap_core(v):
    return lax.ppermute(v, "section", [(0, 1), (1, 0)])


def swap_pair(v):
    return lax.ppermute(v, "row", [(0, 1), (1, 0), (2, 3), (3, 2)])


def gather_tokens(rows):
    return jnp.concatenate(gather4(rows, "z"), axis=0)


def scatter_tokens(partial, beside=None):
    low = partial.astype(bf16)
    n = low.shape[0] // 4
    parts = [low[i * n : (i + 1) * n] for i in range(4)]
    if beside is None:
        return sum4(scatter4(parts, "z"))
    far, near = shift(parts[3], "z", 2), shift(parts[1], "z", 3)
    beside, last = lax.optimization_barrier((beside(), parts[2]))
    return sum4([parts[0], near, shift(last, "z", 1), far]), beside


def dot(a, b):
    return jnp.dot(a, b, preferred_element_type=f32)


def dot_t(a, b):
    return lax.dot_general(a, b, (((1,), (1,)), ((), ())), preferred_element_type=f32)


def t_dot(a, b):
    return lax.dot_general(a, b, (((0,), (0,)), ((), ())), preferred_element_type=f32)


def norm_local(features, gain, bias):
    center = jnp.mean(features, axis=-1, keepdims=True)
    offset = features - center
    spread = jnp.mean(offset * offset, axis=-1, keepdims=True)
    inverse = lax.rsqrt(spread + norm_eps)
    scaled = offset * inverse
    return scaled * gain + bias, scaled, inverse


def norm_back(upstream, scaled, inverse, gain):
    weighted = upstream * gain
    first = jnp.mean(weighted, axis=-1, keepdims=True)
    second = jnp.mean(weighted * scaled, axis=-1, keepdims=True)
    return inverse * (weighted - first - scaled * second)


def gelu_both(v):
    cdf = 0.5 * (1.0 + lax.erf(v * (0.5**0.5)))
    density = jnp.exp(-0.5 * v * v) * 0.3989422804014327
    return (v * cdf).astype(bf16), cdf + v * density


def attend_kernel(q_ref, own_ref, core_ref, pair_ref, both_ref, o_ref, lt_ref):
    q = q_ref[...]
    kv = jnp.concatenate([own_ref[...], core_ref[...], pair_ref[...], both_ref[...]], axis=0)
    s = dot_t(q, kv) * SCALE
    peak = jnp.max(s, axis=-1, keepdims=True)
    raised = jnp.exp(s - peak)
    total = jnp.sum(raised, axis=-1, keepdims=True)
    low = (raised * (1.0 / total)).astype(bf16)
    o = dot(low, kv)
    upper = lax.broadcasted_iota(jnp.int32, o.shape, 1) >= HD
    o_ref[...] = jnp.where(upper, o, 0.0).astype(bf16)
    lt_ref[...] = jnp.broadcast_to(peak + jnp.log(total), lt_ref.shape)


def attend(q, kvs):
    tokens, width = q.shape
    spec = pl.BlockSpec((tokens, 128), lambda h: (0, h))
    return pl.pallas_call(
        attend_kernel,
        grid=(width // 128,),
        in_specs=[spec] * 5,
        out_specs=[spec, spec],
        out_shape=[
            jax.ShapeDtypeStruct((tokens, width), bf16),
            jax.ShapeDtypeStruct((tokens, width), f32),
        ],
        compiler_params=pltpu.CompilerParams(vmem_limit_bytes=32 * 2**20),
        cost_estimate=pl.CostEstimate(flops=4 * 2 * 2 * 256 * 1024 * 128, bytes_accessed=2**21, transcendentals=2**20),
    )(q, *kvs)


def attend_back_kernel(
    q_ref, own_ref, core_ref, pair_ref, both_ref, g_ref, lt_ref, dq_ref, down_ref, dcore_ref, dpair_ref, dboth_ref
):
    q = q_ref[...]
    n = q.shape[0]
    upper = lax.broadcasted_iota(jnp.int32, q.shape, 1) >= HD
    g = jnp.where(upper, g_ref[...], jnp.zeros_like(q))
    kv = jnp.concatenate([own_ref[...], core_ref[...], pair_ref[...], both_ref[...]], axis=0)
    s = dot_t(q, kv) * SCALE
    probs = jnp.exp(s - lt_ref[:, 0:1])
    grad_probs = dot_t(g, kv)
    along = jnp.sum(probs * grad_probs, axis=-1, keepdims=True)
    ds = (probs * (grad_probs - along)).astype(bf16)
    low = probs.astype(bf16)
    dq = dot(ds, kv) * SCALE
    dq_ref[...] = jnp.where(upper, 0.0, dq).astype(bf16)
    dkv = t_dot(ds, q) * SCALE + t_dot(low, g)
    down_ref[...] = dkv[0:n].astype(down_ref.dtype)
    dcore_ref[...] = dkv[n : 2 * n].astype(dcore_ref.dtype)
    dpair_ref[...] = dkv[2 * n : 3 * n].astype(dpair_ref.dtype)
    dboth_ref[...] = dkv[3 * n :].astype(dboth_ref.dtype)


def attend_back(q, kvs, g, lt):
    tokens, width = q.shape
    spec = pl.BlockSpec((tokens, 128), lambda h: (0, h))
    return pl.pallas_call(
        attend_back_kernel,
        grid=(width // 128,),
        in_specs=[spec] * 7,
        out_specs=[spec] * 5,
        out_shape=[
            jax.ShapeDtypeStruct((tokens, width), bf16),
            jax.ShapeDtypeStruct((tokens, width), f32),
            jax.ShapeDtypeStruct((tokens, width), bf16),
            jax.ShapeDtypeStruct((tokens, width), f32),
            jax.ShapeDtypeStruct((tokens, width), bf16),
        ],
        compiler_params=pltpu.CompilerParams(vmem_limit_bytes=40 * 2**20),
        cost_estimate=pl.CostEstimate(flops=4 * 5 * 2 * 256 * 1024 * 128, bytes_accessed=2**22, transcendentals=2**20),
    )(q, *kvs, g, lt)


def tile_of(out_ref, i):
    return out_ref[i] if isinstance(out_ref, tuple) else out_ref.at[i]


def store_sums(out_ref, at, a, b):
    sums = jnp.sum(a[...].astype(f32), axis=0, keepdims=True) + jnp.sum(b[...].astype(f32), axis=0, keepdims=True)
    for i in range(4):
        row = jnp.concatenate([sums[:, i * 128 : (i + 1) * 128], jnp.zeros((1, 128), f32)], axis=1)
        tile_of(out_ref, i)[0, at : at + 16, :] = jnp.broadcast_to(row, (16, 256)).astype(bf16)


def store_tiles(out_ref, at, d):
    for i in range(4):
        tile_of(out_ref, i)[0, at : at + 128, :] = d[i * 128 : (i + 1) * 128].astype(bf16)


def ffn_part(out_ref, at, ge, ge_far, act, act_far, x, x_far, g, g_far):
    store_tiles(out_ref, at, t_dot(ge[...], x[...]) + t_dot(ge_far[...], x_far[...]))
    store_tiles(out_ref, at + 128, t_dot(act[...], g[...]) + t_dot(act_far[...], g_far[...]))
    store_sums(out_ref, at + 256, ge, ge_far)


def att_part(out_ref, at, m, m_far, o, o_far, x, x_far, g, g_far, mask_ref):
    d_proj = t_dot(o[...], g[...]) + t_dot(o_far[...], g_far[...])
    store_tiles(out_ref, at, t_dot(m[...], x[...]) + t_dot(m_far[...], x_far[...]) + mask_ref[...] * d_proj)
    store_sums(out_ref, at + 128, m, m_far)


def ffn_grads_kernel(*refs):
    ffn_part(refs[-1], 0, *refs[:8])


def att_grads_kernel(*refs):
    att_part(refs[-4:], 0, *refs[:9])


def layer_grads_kernel(*refs):
    ffn_part(refs[-1], 0, *refs[:8])
    att_part(refs[-1], 272, *refs[8:17])


def block_grads(kernel, rows, operands, apart=False):
    specs = []
    for v in operands:
        if v.shape[1] == 1024:
            specs.append(pl.BlockSpec((v.shape[0], 256), lambda j: (0, j)))
        else:
            specs.append(pl.BlockSpec(v.shape, lambda j: (0, 0)))
    return pl.pallas_call(
        kernel,
        grid=(4,),
        in_specs=specs,
        out_specs=[pl.BlockSpec((1, rows, 256), lambda j: (j, 0, 0))] * 4
        if apart
        else pl.BlockSpec((4, 1, rows, 256), lambda j: (0, j, 0, 0)),
        out_shape=[jax.ShapeDtypeStruct((4, rows, 256), bf16)] * 4
        if apart
        else jax.ShapeDtypeStruct((4, 4, rows, 256), bf16),
        compiler_params=pltpu.CompilerParams(vmem_limit_bytes=60 * 2**20),
        cost_estimate=pl.CostEstimate(flops=rows * 2**24, bytes_accessed=8 * 2**20, transcendentals=0),
    )(*operands)


def assemble_kernel(first_ref, mine_ref, got_ref, qkv, qb, vb, proj, inner, ib, outer, rows):
    mine, got = mine_ref[...].astype(f32), got_ref[...].astype(f32)
    first = first_ref[0] == 0
    h0, h1 = jnp.where(first, mine, got), jnp.where(first, got, mine)
    inner[...] = jnp.concatenate([h0[0:128], h1[0:128]], axis=0).T
    outer[...] = jnp.concatenate([h0[128:256], h1[128:256]], axis=0)
    ib[...] = jnp.concatenate([h0[256:257, :128], h1[256:257, :128]], axis=1)
    qkv[...] = jnp.concatenate([h1[272:336], h0[272:400]], axis=0)
    proj[...] = h1[336:400]
    qb[...] = h1[400:401, :HD]
    vb[...] = h0[400:401, HD:128]
    rows[...] = h0[416:424] + h1[416:424]


def assemble(first, mine, got):
    shapes = [(192, 256), (1, HD), (1, HD), (64, 256), (256, 256), (1, 256), (256, 256), (8, 256)]
    vmem = pl.BlockSpec(memory_space=pltpu.VMEM)
    return pl.pallas_call(
        assemble_kernel,
        in_specs=[pl.BlockSpec(memory_space=pltpu.SMEM), vmem, vmem],
        out_shape=[jax.ShapeDtypeStruct(v, f32) for v in shapes],
        compiler_params=pltpu.CompilerParams(vmem_limit_bytes=32 * 2**20),
    )(jnp.where(first, 0, 1).astype(jnp.int32).reshape(1), mine, got)


def rows_kernel(direct, a, b, vec, ga, gh, att, gs, n2, gc, g, con, *rest):
    out_ref = rest[-1]
    left = a[...]
    right = b[...] if direct else (b[...].astype(f32) - vec[1:2, :]) * (1.0 / vec[0:1, :])
    out_ref[0:1, :] = jnp.sum(left * right, axis=0, keepdims=True)
    out_ref[1:2, :] = jnp.sum(left, axis=0, keepdims=True)
    out_ref[2:3, :] = jnp.sum(ga[...].astype(f32), axis=0, keepdims=True)
    out_ref[3:4, :] = jnp.sum(gh[...] * att[...], axis=0, keepdims=True)
    out_ref[4:5, :] = jnp.sum(gs[...] * n2[...], axis=0, keepdims=True)
    out_ref[5:6, :] = jnp.sum(gs[...], axis=0, keepdims=True)
    out_ref[6:7, :] = jnp.sum(gc[...].astype(f32), axis=0, keepdims=True)
    if direct:
        total = jnp.sum(rest[0][...].astype(f32) * con[...].astype(f32), axis=0, keepdims=True)
        total = total * (1.0 / vec[7:8, :]) + vec[6:7, :] * jnp.sum(g[...], axis=0, keepdims=True)
        out_ref[7:8, :] = total
    else:
        out_ref[7:8, :] = jnp.sum(g[...] * con[...], axis=0, keepdims=True)


def row_sums(direct, *arrays):
    return pl.pallas_call(
        functools.partial(rows_kernel, direct),
        out_shape=jax.ShapeDtypeStruct((8, 1024), f32),
        compiler_params=pltpu.CompilerParams(vmem_limit_bytes=32 * 2**20),
        cost_estimate=pl.CostEstimate(flops=2**21, bytes_accessed=4 * 2**20, transcendentals=0),
    )(*arrays)


def forward(u, w, beside=None, late=False):
    vec = w["vec"]
    lower = (jnp.arange(512) % 128) < HD
    n1, scaled1, inv1 = norm_local(u, vec[0], vec[1])
    x = gather_tokens(n1.astype(bf16))
    if "att" in w:
        att, x = lax.optimization_barrier((w["att"], x))
        w.update(att_weights(att, w["first"]))
    kv = (dot(x, w["kv"]) + w["kv_bias"]).astype(bf16)
    if beside is not None:
        kv, beside = lax.optimization_barrier((kv, beside))
    kv_pair = swap_pair(kv)
    q = (jnp.where(lower, dot(x, w["qp"]), 0.0) + w["q_bias"]).astype(bf16)
    if beside is not None:
        kv_pair, beside = lax.optimization_barrier((kv_pair, (beside, gather_tokens(beside))))
    kvs = (kv, swap_core(kv), kv_pair, swap_core(kv_pair))
    o, lt = attend(q, kvs)
    attended = scatter_tokens(dot_t(o, w["qp"])) + vec[2]
    hidden = u + vec[3] * attended
    n2, scaled2, inv2 = norm_local(hidden, vec[4], vec[5])
    x2 = gather_tokens(n2.astype(bf16))
    a_own, da_own = gelu_both(dot(x2, w["in_own"]) + w["in_bias_own"])
    a_oth, da_oth = gelu_both(dot(x2, w["in_oth"]) + w["in_bias_oth"])
    partial = (dot_t(a_own, w["out_own"]) + dot_t(a_oth, w["out_oth"])).astype(bf16)
    contracted = partial if late else scatter_tokens(partial) + vec[6]
    one, two = (x, kvs, q, o, lt), (scaled2, inv2, x2, a_own, da_own, a_oth, da_oth)
    return hidden, contracted, (scaled1, inv1, attended), one, two, beside


def reduce_x(blocks):
    return sum4(scatter4(blocks, "x")).astype(bf16)


def reduce_y(blocks):
    return sum4(scatter4(to_slots(blocks), "row")).astype(bf16)


def to_slots(blocks):
    y = lax.axis_index("row")
    return [lax.dynamic_index_in_dim(blocks, (y + k) % 4, 0, keepdims=False) for k in (0, 3, 1, 2)]


def in_order(parts):
    y = lax.axis_index("row")
    stacked = jnp.stack([parts[0], parts[1], parts[3], parts[2]])
    return lax.dynamic_slice_in_dim(jnp.concatenate([stacked, stacked]), (4 - y) % 4, 4, 0)


def backward_ffn(g, gc, gcs, saved, w):
    scaled2, inv2, x2, a_own, da_own, a_oth, da_oth = saved
    ge_own = (dot(gcs, w["out_own"]) * da_own).astype(bf16)
    ge_oth = (dot(gcs, w["out_oth"]) * da_oth).astype(bf16)
    grad_second = scatter_tokens(dot_t(ge_own, w["in_own"]) + dot_t(ge_oth, w["in_oth"]))
    grad_hidden = g + norm_back(grad_second, scaled2, inv2, w["vec"][4])
    ga = (grad_hidden * w["vec"][3]).astype(bf16)
    operands = (ge_own, swap_core(ge_oth), a_own, swap_core(a_oth), x2, swap_core(x2), gcs, swap_core(gcs))
    return grad_hidden, grad_second, ga, operands


def backward_att(gas, saved, w):
    x, kvs, q, o, lt = saved
    gz = dot(gas, w["qp"]).astype(bf16)
    dq, d_own, d_core, d_pair, d_both = attend_back(q, kvs, gz, lt)
    pair_sum = (d_pair + swap_core(d_both).astype(f32)).astype(bf16)
    near = d_own + swap_core(d_core).astype(f32)
    return dq, near, pair_sum


def att_operands(first, dkv, dq, gas, saved):
    x, _, _, o, _ = saved
    return (
        jnp.where(first, dkv, dq),
        swap_core(jnp.where(first, dq, dkv)),
        o,
        swap_core(o),
        x,
        swap_core(x),
        gas,
        swap_core(gas),
        jnp.full((1, 256), jnp.where(first, 0.0, 1.0), f32),
    )


def rows_of(tiles, n):
    return jnp.concatenate([t[:, :n].reshape(-1, t.shape[2]) for t in tiles], axis=1)


def tiles_gathered(half):
    tiles = lax.all_gather(half, ("x", "row"), axis=0, tiled=True).reshape(4, 4, *half.shape)
    return [tiles[i] for i in range(4)]


def split(v):
    high = v.astype(bf16).astype(f32)
    return high, v - high


def cut_weights_kernel(first_ref, qkv_ref, proj_ref, inner_ref, outer_ref, qb, vb, ib, *refs):
    vectors, kept_ref, sent_ref = refs[:8], refs[8], refs[9]
    mine = first_ref[0] == 0
    qkv = qkv_ref[...].astype(f32).T
    outer_t = outer_ref[...].astype(f32).T
    inner = inner_ref[...].astype(f32)
    kv = qkv[:, HD:]
    qp = jnp.concatenate([qkv[:, :HD], proj_ref[...].astype(f32).T], axis=1)
    none = jnp.zeros((1, HD), f32)
    bias0 = jnp.concatenate([none, vb[...], ib[:, :128], none, none], axis=1)
    bias1 = jnp.concatenate([qb[...], none, ib[:, 128:], none, none], axis=1)
    pad = jnp.zeros((14, 384), f32)
    half0 = [jnp.concatenate([kv, inner[:, :128], outer_t[:, :128]], axis=1), *split(bias0), pad]
    half1 = [jnp.concatenate([qp, inner[:, 128:], outer_t[:, 128:]], axis=1), *split(bias1), pad]
    vec = jnp.concatenate(split(jnp.concatenate([v[...] for v in vectors], axis=0)), axis=0)
    vec = jnp.concatenate([vec, jnp.zeros((16, 128), f32)], axis=1)
    half0 = jnp.concatenate([*half0, vec], axis=0)
    half1 = jnp.concatenate([*half1, vec], axis=0)
    kept_ref[...] = jnp.where(mine, half0, half1).astype(bf16)
    sent_ref[...] = jnp.where(mine, half1, half0).astype(bf16)


def cut_weights(first, *arrays):
    place = pl.BlockSpec(memory_space=pltpu.SMEM)
    return pl.pallas_call(
        cut_weights_kernel,
        in_specs=[place] + [pl.BlockSpec(memory_space=pltpu.VMEM)] * len(arrays),
        out_shape=[jax.ShapeDtypeStruct((288, 384), bf16)] * 2,
        compiler_params=pltpu.CompilerParams(vmem_limit_bytes=60 * 2**20),
    )(jnp.where(first, 0, 1).astype(jnp.int32).reshape(1), *arrays)


def joined(rows):
    return rows[0].astype(f32) + rows[1].astype(f32)


def att_weights(att, first):
    far = swap_core(att)
    kv, qp = jnp.where(first, att, far), jnp.where(first, far, att)
    return {"kv": kv[:1024], "qp": qp[:1024], "kv_bias": joined(kv[1024:]), "q_bias": joined(qp[1024:])}


def ffn_weights(tiles, at):
    in_own = rows_of([t[:, :, at : at + 128] for t in tiles], 256)
    out_own = rows_of([t[:, :, at + 128 : at + 256] for t in tiles], 256)
    bias = jnp.concatenate([joined(t[0, 256:258, at : at + 128]) for t in tiles])
    return {
        "in_own": in_own,
        "out_own": out_own,
        "in_oth": swap_core(in_own),
        "out_oth": swap_core(out_own),
        "in_bias_own": bias,
        "in_bias_oth": swap_core(bias),
    }


def sum_over(blocks, axis):
    rows = blocks.reshape(-1, blocks.shape[-1])
    return lax.psum_scatter(rows, axis, scatter_dimension=0, tiled=True).reshape(blocks.shape[1:])


def local(
    block_input,
    cotangent,
    images_used,
    norm1_gain,
    norm1_bias,
    qkv_weight,
    query_bias,
    value_bias,
    proj_weight,
    proj_bias,
    attn_scale,
    norm2_gain,
    norm2_bias,
    inner_weight,
    inner_bias,
    outer_weight,
    outer_bias,
    mlp_scale,
):
    first = lax.axis_index("section") == 0
    y = lax.axis_index("row")

    small = (query_bias, value_bias, inner_bias)
    vectors = (norm1_gain, norm1_bias, proj_bias, attn_scale, norm2_gain, norm2_bias, outer_bias, mlp_scale)
    kept, sent = cut_weights(first, qkv_weight[0].T, proj_weight[0], inner_weight[0], outer_weight[0], *small, *vectors)
    got = swap_core(sent)
    vec_got, got = got[272:, :256], got[:272]
    blocks0, blocks1 = jnp.where(first, kept[:272], got), jnp.where(first, got, kept[:272])
    vec = kept[272:, :256]
    vecs = jnp.concatenate([jnp.where(first, vec, vec_got), jnp.where(first, vec_got, vec)], axis=0)

    tiles = tiles_gathered(jnp.concatenate([blocks0[:, 128:], blocks1], axis=1))

    paired = jnp.stack([block_input, cotangent]).reshape(2, 4, 2, 64, 256)
    paired = jnp.where(first, paired[:, :, 0], paired[:, :, 1])
    shared = jnp.concatenate([vecs, jnp.concatenate([blocks0[:128, :128], blocks0[128:256, :128]], axis=1)], axis=0)
    messages = []
    paired = lax.dynamic_slice_in_dim(jnp.concatenate([paired, paired], axis=1), y, 4, 1)
    for k in (0, 3, 1, 2):
        messages.append(jnp.concatenate([paired[0, k], paired[1, k], shared], axis=0))
    got = scatter4(messages, "row")
    ordered = jnp.stack([got[0], got[1], got[3], got[2]])
    ordered = lax.dynamic_slice_in_dim(jnp.concatenate([ordered, ordered]), (4 - y) % 4, 4, 0)
    tokens = jnp.concatenate([ordered[i, :128] for i in range(4)], axis=1).astype(f32)
    vecs = jnp.concatenate([ordered[i, 128:160] for i in range(4)], axis=1).astype(f32)
    att = jnp.concatenate([ordered[:, 160:, :128], ordered[:, 160:, 128:]], axis=1).reshape(1024, 128)
    att = jnp.concatenate([att, blocks0[256:264, :128]], axis=0)
    att = jnp.concatenate(gather4(att, "x"), axis=1)

    tiles_att1 = [t[:, :, 256:384] for t in tiles]
    att1 = jnp.concatenate([rows_of(tiles_att1, 256), jnp.concatenate([t[0, 256:264] for t in tiles_att1], axis=1)])
    w0 = {"vec": vecs[0:8] + vecs[8:16], "att": att, "first": first, **ffn_weights(tiles, 0)}
    w1 = {"vec": vecs[16:24] + vecs[24:32], **att_weights(att1, first), **ffn_weights(tiles, 384)}

    used = jnp.where(y < 2, images_used[0], images_used[1])
    live = (lax.axis_index("x") < used).astype(f32)

    seed = live * tokens[64:]
    vec0, vec1 = w0["vec"], w1["vec"]
    seed_low = (seed * vec1[7]).astype(bf16)
    hidden0, contracted0, norm0, one0, two0, gcs1 = forward(tokens[:64], w0, seed_low)
    seed_low, gcs1 = gcs1
    handed = (hidden0 + vec0[7] * contracted0).astype(bf16).astype(f32)
    hidden1, contracted1, norm1, one1, two1, _ = forward(handed, w1, None, True)


    grad_hidden1, grad_second1, ga1, ffn1 = backward_ffn(seed, seed_low, gcs1, two1, w1)
    gas1 = gather_tokens(ga1)
    dq1, near1, pair1 = backward_att(gas1, one1, w1)
    dkv1 = (near1 + swap_pair(pair1).astype(f32)).astype(bf16)
    partial1 = dot_t(dkv1, w1["kv"]) + dot_t(dq1, w1["qp"])
    grad_normed1, blocks1 = scatter_tokens(partial1, lambda: block_grads(ffn_grads_kernel, 272, ffn1))
    blocks1 = sum_over(blocks1, "x")
    att1 = att_operands(first, dkv1, dq1, gas1, one1)
    back1 = grad_hidden1 + norm_back(grad_normed1, norm1[0], norm1[1], vec1[0])
    g0 = back1.astype(bf16).astype(f32)

    gc0 = (g0 * vec0[7]).astype(bf16)
    gcs0 = gather_tokens(gc0)
    grad_hidden0, grad_second0, ga0, ffn0 = backward_ffn(g0, gc0, gcs0, two0, w0)
    gas0 = gather_tokens(ga0)
    dq0, near0, pair0 = backward_att(gas0, one0, w0)
    mixed = sum_over(block_grads(layer_grads_kernel, 416, ffn0 + att1), "x")
    dkv0 = (near0 + swap_pair(pair0).astype(f32)).astype(bf16)
    partial0 = dot_t(dkv0, w0["kv"]) + dot_t(dq0, w0["qp"])
    partial0, mixed = lax.optimization_barrier((partial0, mixed))
    mixed, blocks1 = sum_over(mixed, "row"), sum_over(blocks1, "row")
    rows1 = row_sums(
        True, grad_normed1, norm1[0], vec1, ga1, grad_hidden1, norm1[2], grad_second1, two1[0], seed_low, seed, contracted1, gcs1
    )
    att0 = att_operands(first, dkv0, dq0, gas0, one0)
    rows0 = row_sums(
        False, partial0, one0[0], vec0, ga0, grad_hidden0, norm0[2], grad_second0, two0[0], gc0, g0, contracted0
    )
    att0 = block_grads(att_grads_kernel, 144, att0, True)
    low, att0 = lax.optimization_barrier((partial0.astype(bf16), att0))
    rows0 = jnp.concatenate([rows0, rows1], axis=0).astype(bf16)
    cuts = [slice(i * 64, (i + 1) * 64) for i in range(4)]
    parts = scatter4([jnp.concatenate([low[c], rows0, contracted1[c]], axis=0) for c in cuts], "z")
    contracted1 = sum4([p[80:] for p in parts]) + vec1[6]
    final = (live * (hidden1 + vec1[7] * contracted1)).astype(bf16)
    att0 = reduce_x(att0)
    grad_normed0, rows0 = sum4([p[:64] for p in parts]), sum4([p[64:80] for p in parts])
    rows = sum4(gather4(rows0.astype(bf16), "x")).astype(bf16)
    grad_in = (grad_hidden0 + norm_back(grad_normed0, norm0[0], norm0[1], vec0[0])).astype(bf16)

    own = jnp.where(first, grad_in, final)
    got = swap_core(jnp.where(first, final, grad_in))
    edge = jnp.concatenate([jnp.where(first, own, got), jnp.where(first, got, own), rows], axis=0)
    edge = jnp.stack([edge[:, i * 256 : (i + 1) * 256] for i in range(4)])
    got = scatter4(to_slots(jnp.concatenate([edge, att0], axis=1)), "row")
    got, mixed, blocks1 = lax.optimization_barrier((got, mixed, blocks1))
    edge = in_order([p[:128] for p in got]).reshape(1, 2, 256, 256).astype(f32)
    rest = sum4([p[128:] for p in got]).astype(bf16)

    layer0 = jnp.concatenate([mixed[:272], rest[16:], rest[:8]], axis=0)
    layer1 = jnp.concatenate([blocks1, mixed[272:], rest[8:16]], axis=0)
    far = swap_core(jnp.where(first, layer1, layer0))
    qkv, qb, vb, proj, inner, ib, outer, rows = assemble(first, jnp.where(first, layer0, layer1), far)

    return (
        edge,
        rows[0][None],
        rows[1][None],
        qkv.T[None],
        qb,
        vb,
        proj[None],
        rows[2][None],
        rows[3][None],
        rows[4][None],
        rows[5][None],
        inner[None],
        ib,
        outer[None],
        rows[6][None],
        rows[7][None],
    )


def solution(mesh):
    grid = Mesh(mesh.devices.reshape(2, 4, 4, 4), ("section", "row", "x", "z"))
    col = ("x", "z")
    by_row = P("section", "row")
    by_col = P("section", col)
    matrix = P("section", "row", col)
    matrix_t = P("section", col, "row")
    return jax.shard_map(
        local,
        mesh=grid,
        in_specs=(
            P(None, col, "row"),
            P(None, col, "row"),
            P(),
            by_row,
            by_row,
            matrix,
            by_col,
            by_col,
            matrix_t,
            by_row,
            by_row,
            by_row,
            by_row,
            matrix,
            by_col,
            matrix_t,
            by_row,
            by_row,
        ),
        out_specs=(
            P("section", None, col, "row"),
            by_row,
            by_row,
            matrix,
            by_col,
            by_col,
            matrix_t,
            by_row,
            by_row,
            by_row,
            by_row,
            matrix,
            by_col,
            matrix_t,
            by_row,
            by_row,
        ),
        check_vma=False,
    )
```

```python
import functools

import jax
import jax.numpy as jnp
from jax import lax
from jax.experimental import pallas as pl
from jax.experimental.pallas import tpu as pltpu
from jax.sharding import Mesh
from jax.sharding import PartitionSpec as P

HD = 64
norm_eps = 1e-06
bf16 = jnp.bfloat16
f32 = jnp.float32
SCALE = HD ** (-0.5)


def shift(v, axis, by):
    return lax.ppermute(v, axis, [(i, (i + by) % 4) for i in range(4)])


def gather4(v, axis):
    far = shift(v, axis, 2)
    return [v, shift(v, axis, 1), shift(v, axis, 3), far]


def scatter4(parts, axis):
    far = shift(parts[3], axis, 2)
    return [parts[0], shift(parts[1], axis, 3), shift(parts[2], axis, 1), far]


def sum4(parts):
    a, b, c, d = [p.astype(f32) for p in parts]
    return (a + b) + (c + d)


def swap_core(v):
    return lax.ppermute(v, "section", [(0, 1), (1, 0)])


def swap_pair(v):
    return lax.ppermute(v, "row", [(0, 1), (1, 0), (2, 3), (3, 2)])


def gather_tokens(rows):
    return jnp.concatenate(gather4(rows, "z"), axis=0)


def scatter_tokens(partial, beside=None):
    low = partial.astype(bf16)
    n = low.shape[0] // 4
    parts = [low[i * n : (i + 1) * n] for i in range(4)]
    if beside is None:
        return sum4(scatter4(parts, "z"))
    far, near = shift(parts[3], "z", 2), shift(parts[1], "z", 3)
    beside, last = lax.optimization_barrier((beside(), parts[2]))
    return sum4([parts[0], near, shift(last, "z", 1), far]), beside


def dot(a, b):
    return jnp.dot(a, b, preferred_element_type=f32)


def dot_t(a, b):
    return lax.dot_general(a, b, (((1,), (1,)), ((), ())), preferred_element_type=f32)


def t_dot(a, b):
    return lax.dot_general(a, b, (((0,), (0,)), ((), ())), preferred_element_type=f32)


def norm_local(features, gain, bias):
    center = jnp.mean(features, axis=-1, keepdims=True)
    offset = features - center
    spread = jnp.mean(offset * offset, axis=-1, keepdims=True)
    inverse = lax.rsqrt(spread + norm_eps)
    scaled = offset * inverse
    return scaled * gain + bias, scaled, inverse


def norm_back(upstream, scaled, inverse, gain):
    weighted = upstream * gain
    first = jnp.mean(weighted, axis=-1, keepdims=True)
    second = jnp.mean(weighted * scaled, axis=-1, keepdims=True)
    return inverse * (weighted - first - scaled * second)


def gelu_both(v):
    cdf = 0.5 * (1.0 + lax.erf(v * (0.5**0.5)))
    density = jnp.exp(-0.5 * v * v) * 0.3989422804014327
    return (v * cdf).astype(bf16), cdf + v * density


def attend_kernel(q_ref, own_ref, core_ref, pair_ref, both_ref, o_ref, lt_ref):
    q = q_ref[...]
    kv = jnp.concatenate([own_ref[...], core_ref[...], pair_ref[...], both_ref[...]], axis=0)
    s = dot_t(q, kv) * SCALE
    peak = jnp.max(s, axis=-1, keepdims=True)
    raised = jnp.exp(s - peak)
    total = jnp.sum(raised, axis=-1, keepdims=True)
    low = (raised * (1.0 / total)).astype(bf16)
    o = dot(low, kv)
    upper = lax.broadcasted_iota(jnp.int32, o.shape, 1) >= HD
    o_ref[...] = jnp.where(upper, o, 0.0).astype(bf16)
    lt_ref[...] = jnp.broadcast_to(peak + jnp.log(total), lt_ref.shape)


def attend(q, kvs):
    tokens, width = q.shape
    spec = pl.BlockSpec((tokens, 128), lambda h: (0, h))
    return pl.pallas_call(
        attend_kernel,
        grid=(width // 128,),
        in_specs=[spec] * 5,
        out_specs=[spec, spec],
        out_shape=[
            jax.ShapeDtypeStruct((tokens, width), bf16),
            jax.ShapeDtypeStruct((tokens, width), f32),
        ],
        compiler_params=pltpu.CompilerParams(vmem_limit_bytes=32 * 2**20),
        cost_estimate=pl.CostEstimate(flops=4 * 2 * 2 * 256 * 1024 * 128, bytes_accessed=2**21, transcendentals=2**20),
    )(q, *kvs)


def attend_back_kernel(
    q_ref, own_ref, core_ref, pair_ref, both_ref, g_ref, lt_ref, dq_ref, down_ref, dcore_ref, dpair_ref, dboth_ref
):
    q = q_ref[...]
    n = q.shape[0]
    upper = lax.broadcasted_iota(jnp.int32, q.shape, 1) >= HD
    g = jnp.where(upper, g_ref[...], jnp.zeros_like(q))
    kv = jnp.concatenate([own_ref[...], core_ref[...], pair_ref[...], both_ref[...]], axis=0)
    s = dot_t(q, kv) * SCALE
    probs = jnp.exp(s - lt_ref[:, 0:1])
    grad_probs = dot_t(g, kv)
    along = jnp.sum(probs * grad_probs, axis=-1, keepdims=True)
    ds = (probs * (grad_probs - along)).astype(bf16)
    low = probs.astype(bf16)
    dq = dot(ds, kv) * SCALE
    dq_ref[...] = jnp.where(upper, 0.0, dq).astype(bf16)
    dkv = t_dot(ds, q) * SCALE + t_dot(low, g)
    down_ref[...] = dkv[0:n].astype(down_ref.dtype)
    dcore_ref[...] = dkv[n : 2 * n].astype(dcore_ref.dtype)
    dpair_ref[...] = dkv[2 * n : 3 * n].astype(dpair_ref.dtype)
    dboth_ref[...] = dkv[3 * n :].astype(dboth_ref.dtype)


def attend_back(q, kvs, g, lt):
    tokens, width = q.shape
    spec = pl.BlockSpec((tokens, 128), lambda h: (0, h))
    return pl.pallas_call(
        attend_back_kernel,
        grid=(width // 128,),
        in_specs=[spec] * 7,
        out_specs=[spec] * 5,
        out_shape=[
            jax.ShapeDtypeStruct((tokens, width), bf16),
            jax.ShapeDtypeStruct((tokens, width), f32),
            jax.ShapeDtypeStruct((tokens, width), bf16),
            jax.ShapeDtypeStruct((tokens, width), f32),
            jax.ShapeDtypeStruct((tokens, width), bf16),
        ],
        compiler_params=pltpu.CompilerParams(vmem_limit_bytes=40 * 2**20),
        cost_estimate=pl.CostEstimate(flops=4 * 5 * 2 * 256 * 1024 * 128, bytes_accessed=2**22, transcendentals=2**20),
    )(q, *kvs, g, lt)


def tile_of(out_ref, i):
    return out_ref[i] if isinstance(out_ref, tuple) else out_ref.at[i]


def store_sums(out_ref, at, a, b):
    sums = jnp.sum(a[...].astype(f32), axis=0, keepdims=True) + jnp.sum(b[...].astype(f32), axis=0, keepdims=True)
    for i in range(4):
        row = jnp.concatenate([sums[:, i * 128 : (i + 1) * 128], jnp.zeros((1, 128), f32)], axis=1)
        tile_of(out_ref, i)[0, at : at + 16, :] = jnp.broadcast_to(row, (16, 256)).astype(bf16)


def store_tiles(out_ref, at, d):
    for i in range(4):
        tile_of(out_ref, i)[0, at : at + 128, :] = d[i * 128 : (i + 1) * 128].astype(bf16)


def ffn_part(out_ref, at, ge, ge_far, act, act_far, x, x_far, g, g_far):
    store_tiles(out_ref, at, t_dot(ge[...], x[...]) + t_dot(ge_far[...], x_far[...]))
    store_tiles(out_ref, at + 128, t_dot(act[...], g[...]) + t_dot(act_far[...], g_far[...]))
    store_sums(out_ref, at + 256, ge, ge_far)


def att_part(out_ref, at, m, m_far, o, o_far, x, x_far, g, g_far, mask_ref):
    d_proj = t_dot(o[...], g[...]) + t_dot(o_far[...], g_far[...])
    store_tiles(out_ref, at, t_dot(m[...], x[...]) + t_dot(m_far[...], x_far[...]) + mask_ref[...] * d_proj)
    store_sums(out_ref, at + 128, m, m_far)


def ffn_grads_kernel(*refs):
    ffn_part(refs[-1], 0, *refs[:8])


def att_grads_kernel(*refs):
    att_part(refs[-4:], 0, *refs[:9])


def layer_grads_kernel(*refs):
    ffn_part(refs[-1], 0, *refs[:8])
    att_part(refs[-1], 272, *refs[8:17])


def block_grads(kernel, rows, operands, apart=False):
    specs = []
    for v in operands:
        if v.shape[1] == 1024:
            specs.append(pl.BlockSpec((v.shape[0], 256), lambda j: (0, j)))
        else:
            specs.append(pl.BlockSpec(v.shape, lambda j: (0, 0)))
    return pl.pallas_call(
        kernel,
        grid=(4,),
        in_specs=specs,
        out_specs=[pl.BlockSpec((1, rows, 256), lambda j: (j, 0, 0))] * 4
        if apart
        else pl.BlockSpec((4, 1, rows, 256), lambda j: (0, j, 0, 0)),
        out_shape=[jax.ShapeDtypeStruct((4, rows, 256), bf16)] * 4
        if apart
        else jax.ShapeDtypeStruct((4, 4, rows, 256), bf16),
        compiler_params=pltpu.CompilerParams(vmem_limit_bytes=60 * 2**20),
        cost_estimate=pl.CostEstimate(flops=rows * 2**24, bytes_accessed=8 * 2**20, transcendentals=0),
    )(*operands)


def assemble_kernel(first_ref, mine_ref, got_ref, qkv, qb, vb, proj, inner, ib, outer, rows):
    mine, got = mine_ref[...].astype(f32), got_ref[...].astype(f32)
    first = first_ref[0] == 0
    h0, h1 = jnp.where(first, mine, got), jnp.where(first, got, mine)
    inner[...] = jnp.concatenate([h0[0:128], h1[0:128]], axis=0).T
    outer[...] = jnp.concatenate([h0[128:256], h1[128:256]], axis=0)
    ib[...] = jnp.concatenate([h0[256:257, :128], h1[256:257, :128]], axis=1)
    qkv[...] = jnp.concatenate([h1[272:336], h0[272:400]], axis=0)
    proj[...] = h1[336:400]
    qb[...] = h1[400:401, :HD]
    vb[...] = h0[400:401, HD:128]
    rows[...] = h0[416:424] + h1[416:424]


def assemble(first, mine, got):
    shapes = [(192, 256), (1, HD), (1, HD), (64, 256), (256, 256), (1, 256), (256, 256), (8, 256)]
    vmem = pl.BlockSpec(memory_space=pltpu.VMEM)
    return pl.pallas_call(
        assemble_kernel,
        in_specs=[pl.BlockSpec(memory_space=pltpu.SMEM), vmem, vmem],
        out_shape=[jax.ShapeDtypeStruct(v, f32) for v in shapes],
        compiler_params=pltpu.CompilerParams(vmem_limit_bytes=32 * 2**20),
    )(jnp.where(first, 0, 1).astype(jnp.int32).reshape(1), mine, got)


def rows_kernel(direct, a, b, vec, ga, gh, att, gs, n2, gc, g, con, *rest):
    out_ref = rest[-1]
    left = a[...]
    right = b[...] if direct else (b[...].astype(f32) - vec[1:2, :]) * (1.0 / vec[0:1, :])
    out_ref[0:1, :] = jnp.sum(left * right, axis=0, keepdims=True)
    out_ref[1:2, :] = jnp.sum(left, axis=0, keepdims=True)
    out_ref[2:3, :] = jnp.sum(ga[...].astype(f32), axis=0, keepdims=True)
    out_ref[3:4, :] = jnp.sum(gh[...] * att[...], axis=0, keepdims=True)
    out_ref[4:5, :] = jnp.sum(gs[...] * n2[...], axis=0, keepdims=True)
    out_ref[5:6, :] = jnp.sum(gs[...], axis=0, keepdims=True)
    out_ref[6:7, :] = jnp.sum(gc[...].astype(f32), axis=0, keepdims=True)
    if direct:
        total = jnp.sum(rest[0][...].astype(f32) * con[...].astype(f32), axis=0, keepdims=True)
        total = total * (1.0 / vec[7:8, :]) + vec[6:7, :] * jnp.sum(g[...], axis=0, keepdims=True)
        out_ref[7:8, :] = total
    else:
        out_ref[7:8, :] = jnp.sum(g[...] * con[...], axis=0, keepdims=True)


def row_sums(direct, *arrays):
    return pl.pallas_call(
        functools.partial(rows_kernel, direct),
        out_shape=jax.ShapeDtypeStruct((8, 1024), f32),
        compiler_params=pltpu.CompilerParams(vmem_limit_bytes=32 * 2**20),
        cost_estimate=pl.CostEstimate(flops=2**21, bytes_accessed=4 * 2**20, transcendentals=0),
    )(*arrays)


def forward(u, w, beside=None, late=False):
    vec = w["vec"]
    lower = (jnp.arange(512) % 128) < HD
    n1, scaled1, inv1 = norm_local(u, vec[0], vec[1])
    x = gather_tokens(n1.astype(bf16))
    if "att" in w:
        att, x = lax.optimization_barrier((w["att"], x))
        w.update(att_weights(att, w["first"]))
    kv = (dot(x, w["kv"]) + w["kv_bias"]).astype(bf16)
    if beside is not None:
        kv, beside = lax.optimization_barrier((kv, beside))
    kv_pair = swap_pair(kv)
    q = (jnp.where(lower, dot(x, w["qp"]), 0.0) + w["q_bias"]).astype(bf16)
    if beside is not None:
        kv_pair, beside = lax.optimization_barrier((kv_pair, (beside, gather_tokens(beside))))
    kvs = (kv, swap_core(kv), kv_pair, swap_core(kv_pair))
    o, lt = attend(q, kvs)
    attended = scatter_tokens(dot_t(o, w["qp"])) + vec[2]
    hidden = u + vec[3] * attended
    n2, scaled2, inv2 = norm_local(hidden, vec[4], vec[5])
    x2 = gather_tokens(n2.astype(bf16))
    a_own, da_own = gelu_both(dot(x2, w["in_own"]) + w["in_bias_own"])
    a_oth, da_oth = gelu_both(dot(x2, w["in_oth"]) + w["in_bias_oth"])
    partial = (dot_t(a_own, w["out_own"]) + dot_t(a_oth, w["out_oth"])).astype(bf16)
    contracted = partial if late else scatter_tokens(partial) + vec[6]
    one, two = (x, kvs, q, o, lt), (scaled2, inv2, x2, a_own, da_own, a_oth, da_oth)
    return hidden, contracted, (scaled1, inv1, attended), one, two, beside


def reduce_x(blocks):
    return sum4(scatter4(blocks, "x")).astype(bf16)


def reduce_y(blocks):
    return sum4(scatter4(to_slots(blocks), "row")).astype(bf16)


def to_slots(blocks):
    y = lax.axis_index("row")
    return [lax.dynamic_index_in_dim(blocks, (y + k) % 4, 0, keepdims=False) for k in (0, 3, 1, 2)]


def in_order(parts):
    y = lax.axis_index("row")
    stacked = jnp.stack([parts[0], parts[1], parts[3], parts[2]])
    return lax.dynamic_slice_in_dim(jnp.concatenate([stacked, stacked]), (4 - y) % 4, 4, 0)


def backward_ffn(g, gc, gcs, saved, w):
    scaled2, inv2, x2, a_own, da_own, a_oth, da_oth = saved
    ge_own = (dot(gcs, w["out_own"]) * da_own).astype(bf16)
    ge_oth = (dot(gcs, w["out_oth"]) * da_oth).astype(bf16)
    grad_second = scatter_tokens(dot_t(ge_own, w["in_own"]) + dot_t(ge_oth, w["in_oth"]))
    grad_hidden = g + norm_back(grad_second, scaled2, inv2, w["vec"][4])
    ga = (grad_hidden * w["vec"][3]).astype(bf16)
    operands = (ge_own, swap_core(ge_oth), a_own, swap_core(a_oth), x2, swap_core(x2), gcs, swap_core(gcs))
    return grad_hidden, grad_second, ga, operands


def backward_att(gas, saved, w):
    x, kvs, q, o, lt = saved
    gz = dot(gas, w["qp"]).astype(bf16)
    dq, d_own, d_core, d_pair, d_both = attend_back(q, kvs, gz, lt)
    pair_sum = (d_pair + swap_core(d_both).astype(f32)).astype(bf16)
    near = d_own + swap_core(d_core).astype(f32)
    return dq, near, pair_sum


def att_operands(first, dkv, dq, gas, saved):
    x, _, _, o, _ = saved
    return (
        jnp.where(first, dkv, dq),
        swap_core(jnp.where(first, dq, dkv)),
        o,
        swap_core(o),
        x,
        swap_core(x),
        gas,
        swap_core(gas),
        jnp.full((1, 256), jnp.where(first, 0.0, 1.0), f32),
    )


def rows_of(tiles, n):
    return jnp.concatenate([t[:, :n].reshape(-1, t.shape[2]) for t in tiles], axis=1)


def tiles_gathered(half):
    tiles = lax.all_gather(half, ("x", "row"), axis=0, tiled=True).reshape(4, 4, *half.shape)
    return [tiles[i] for i in range(4)]


def split(v):
    high = v.astype(bf16).astype(f32)
    return high, v - high


def cut_weights_kernel(first_ref, qkv_ref, proj_ref, inner_ref, outer_ref, qb, vb, ib, *refs):
    vectors, kept_ref, sent_ref = refs[:8], refs[8], refs[9]
    mine = first_ref[0] == 0
    qkv = qkv_ref[...].astype(f32).T
    outer_t = outer_ref[...].astype(f32).T
    inner = inner_ref[...].astype(f32)
    kv = qkv[:, HD:]
    qp = jnp.concatenate([qkv[:, :HD], proj_ref[...].astype(f32).T], axis=1)
    none = jnp.zeros((1, HD), f32)
    bias0 = jnp.concatenate([none, vb[...], ib[:, :128], none, none], axis=1)
    bias1 = jnp.concatenate([qb[...], none, ib[:, 128:], none, none], axis=1)
    pad = jnp.zeros((14, 384), f32)
    half0 = [jnp.concatenate([kv, inner[:, :128], outer_t[:, :128]], axis=1), *split(bias0), pad]
    half1 = [jnp.concatenate([qp, inner[:, 128:], outer_t[:, 128:]], axis=1), *split(bias1), pad]
    vec = jnp.concatenate(split(jnp.concatenate([v[...] for v in vectors], axis=0)), axis=0)
    vec = jnp.concatenate([vec, jnp.zeros((16, 128), f32)], axis=1)
    half0 = jnp.concatenate([*half0, vec], axis=0)
    half1 = jnp.concatenate([*half1, vec], axis=0)
    kept_ref[...] = jnp.where(mine, half0, half1).astype(bf16)
    sent_ref[...] = jnp.where(mine, half1, half0).astype(bf16)


def cut_weights(first, *arrays):
    place = pl.BlockSpec(memory_space=pltpu.SMEM)
    return pl.pallas_call(
        cut_weights_kernel,
        in_specs=[place] + [pl.BlockSpec(memory_space=pltpu.VMEM)] * len(arrays),
        out_shape=[jax.ShapeDtypeStruct((288, 384), bf16)] * 2,
        compiler_params=pltpu.CompilerParams(vmem_limit_bytes=60 * 2**20),
    )(jnp.where(first, 0, 1).astype(jnp.int32).reshape(1), *arrays)


def joined(rows):
    return rows[0].astype(f32) + rows[1].astype(f32)


def att_weights(att, first):
    far = swap_core(att)
    kv, qp = jnp.where(first, att, far), jnp.where(first, far, att)
    return {"kv": kv[:1024], "qp": qp[:1024], "kv_bias": joined(kv[1024:]), "q_bias": joined(qp[1024:])}


def ffn_weights(tiles, at):
    in_own = rows_of([t[:, :, at : at + 128] for t in tiles], 256)
    out_own = rows_of([t[:, :, at + 128 : at + 256] for t in tiles], 256)
    bias = jnp.concatenate([joined(t[0, 256:258, at : at + 128]) for t in tiles])
    return {
        "in_own": in_own,
        "out_own": out_own,
        "in_oth": swap_core(in_own),
        "out_oth": swap_core(out_own),
        "in_bias_own": bias,
        "in_bias_oth": swap_core(bias),
    }


def sum_over(blocks, axis):
    rows = blocks.reshape(-1, blocks.shape[-1])
    return lax.psum_scatter(rows, axis, scatter_dimension=0, tiled=True).reshape(blocks.shape[1:])


def local(
    block_input,
    cotangent,
    images_used,
    norm1_gain,
    norm1_bias,
    qkv_weight,
    query_bias,
    value_bias,
    proj_weight,
    proj_bias,
    attn_scale,
    norm2_gain,
    norm2_bias,
    inner_weight,
    inner_bias,
    outer_weight,
    outer_bias,
    mlp_scale,
):
    first = lax.axis_index("section") == 0
    y = lax.axis_index("row")

    small = (query_bias, value_bias, inner_bias)
    vectors = (norm1_gain, norm1_bias, proj_bias, attn_scale, norm2_gain, norm2_bias, outer_bias, mlp_scale)
    kept, sent = cut_weights(first, qkv_weight[0].T, proj_weight[0], inner_weight[0], outer_weight[0], *small, *vectors)
    got = swap_core(sent)
    vec_got, got = got[272:, :256], got[:272]
    blocks0, blocks1 = jnp.where(first, kept[:272], got), jnp.where(first, got, kept[:272])
    vec = kept[272:, :256]
    vecs = jnp.concatenate([jnp.where(first, vec, vec_got), jnp.where(first, vec_got, vec)], axis=0)

    tiles = tiles_gathered(jnp.concatenate([blocks0[:, 128:], blocks1], axis=1))

    paired = jnp.stack([block_input, cotangent]).reshape(2, 4, 2, 64, 256)
    paired = jnp.where(first, paired[:, :, 0], paired[:, :, 1])
    shared = jnp.concatenate([vecs, jnp.concatenate([blocks0[:128, :128], blocks0[128:256, :128]], axis=1)], axis=0)
    messages = []
    paired = lax.dynamic_slice_in_dim(jnp.concatenate([paired, paired], axis=1), y, 4, 1)
    for k in (0, 3, 1, 2):
        messages.append(jnp.concatenate([paired[0, k], paired[1, k], shared], axis=0))
    got = scatter4(messages, "row")
    ordered = jnp.stack([got[0], got[1], got[3], got[2]])
    ordered = lax.dynamic_slice_in_dim(jnp.concatenate([ordered, ordered]), (4 - y) % 4, 4, 0)
    tokens = jnp.concatenate([ordered[i, :128] for i in range(4)], axis=1).astype(f32)
    vecs = jnp.concatenate([ordered[i, 128:160] for i in range(4)], axis=1).astype(f32)
    att = jnp.concatenate([ordered[:, 160:, :128], ordered[:, 160:, 128:]], axis=1).reshape(1024, 128)
    att = jnp.concatenate([att, blocks0[256:264, :128]], axis=0)
    att = jnp.concatenate(gather4(att, "x"), axis=1)

    tiles_att1 = [t[:, :, 256:384] for t in tiles]
    att1 = jnp.concatenate([rows_of(tiles_att1, 256), jnp.concatenate([t[0, 256:264] for t in tiles_att1], axis=1)])
    w0 = {"vec": vecs[0:8] + vecs[8:16], "att": att, "first": first, **ffn_weights(tiles, 0)}
    w1 = {"vec": vecs[16:24] + vecs[24:32], **att_weights(att1, first), **ffn_weights(tiles, 384)}

    used = jnp.where(y < 2, images_used[0], images_used[1])
    live = (lax.axis_index("x") < used).astype(f32)

    seed = live * tokens[64:]
    vec0, vec1 = w0["vec"], w1["vec"]
    seed_low = (seed * vec1[7]).astype(bf16)
    hidden0, contracted0, norm0, one0, two0, gcs1 = forward(tokens[:64], w0, seed_low)
    seed_low, gcs1 = gcs1
    handed = (hidden0 + vec0[7] * contracted0).astype(bf16).astype(f32)
    hidden1, contracted1, norm1, one1, two1, _ = forward(handed, w1, None, True)


    grad_hidden1, grad_second1, ga1, ffn1 = backward_ffn(seed, seed_low, gcs1, two1, w1)
    gas1 = gather_tokens(ga1)
    dq1, near1, pair1 = backward_att(gas1, one1, w1)
    dkv1 = (near1 + swap_pair(pair1).astype(f32)).astype(bf16)
    partial1 = dot_t(dkv1, w1["kv"]) + dot_t(dq1, w1["qp"])
    grad_normed1, blocks1 = scatter_tokens(partial1, lambda: block_grads(ffn_grads_kernel, 272, ffn1))
    blocks1 = sum_over(blocks1, "x")
    att1 = att_operands(first, dkv1, dq1, gas1, one1)
    back1 = grad_hidden1 + norm_back(grad_normed1, norm1[0], norm1[1], vec1[0])
    g0 = back1.astype(bf16).astype(f32)

    gc0 = (g0 * vec0[7]).astype(bf16)
    gcs0 = gather_tokens(gc0)
    grad_hidden0, grad_second0, ga0, ffn0 = backward_ffn(g0, gc0, gcs0, two0, w0)
    gas0 = gather_tokens(ga0)
    dq0, near0, pair0 = backward_att(gas0, one0, w0)
    mixed = sum_over(block_grads(layer_grads_kernel, 416, ffn0 + att1), "x")
    rows1 = row_sums(
        True, grad_normed1, norm1[0], vec1, ga1, grad_hidden1, norm1[2], grad_second1, two1[0], seed_low, seed, contracted1, gcs1
    )
    pair0, rows1 = lax.optimization_barrier((swap_pair(pair0), rows1.astype(bf16)))
    dkv0 = (near0 + pair0.astype(f32)).astype(bf16)
    partial0 = dot_t(dkv0, w0["kv"]) + dot_t(dq0, w0["qp"])
    partial0, mixed = lax.optimization_barrier((partial0, mixed))
    mixed, blocks1 = sum_over(mixed, "row"), sum_over(blocks1, "row")
    att0 = att_operands(first, dkv0, dq0, gas0, one0)
    rows0 = row_sums(
        False, partial0, one0[0], vec0, ga0, grad_hidden0, norm0[2], grad_second0, two0[0], gc0, g0, contracted0
    )
    att0 = block_grads(att_grads_kernel, 144, att0, True)
    low, att0 = lax.optimization_barrier((partial0.astype(bf16), att0))
    rows0 = jnp.concatenate([rows0.astype(bf16), rows1], axis=0)
    cuts = [slice(i * 64, (i + 1) * 64) for i in range(4)]
    parts = scatter4([jnp.concatenate([low[c], rows0, contracted1[c]], axis=0) for c in cuts], "z")
    contracted1 = sum4([p[80:] for p in parts]) + vec1[6]
    final = (live * (hidden1 + vec1[7] * contracted1)).astype(bf16)
    att0 = reduce_x(att0)
    grad_normed0, rows0 = sum4([p[:64] for p in parts]), sum4([p[64:80] for p in parts])
    rows = sum4(gather4(rows0.astype(bf16), "x")).astype(bf16)
    grad_in = (grad_hidden0 + norm_back(grad_normed0, norm0[0], norm0[1], vec0[0])).astype(bf16)

    own = jnp.where(first, grad_in, final)
    got = swap_core(jnp.where(first, final, grad_in))
    edge = jnp.concatenate([jnp.where(first, own, got), jnp.where(first, got, own), rows], axis=0)
    edge = jnp.stack([edge[:, i * 256 : (i + 1) * 256] for i in range(4)])
    got = scatter4(to_slots(jnp.concatenate([edge, att0], axis=1)), "row")
    got, mixed, blocks1 = lax.optimization_barrier((got, mixed, blocks1))
    edge = in_order([p[:128] for p in got]).reshape(1, 2, 256, 256).astype(f32)
    rest = sum4([p[128:] for p in got]).astype(bf16)

    layer0 = jnp.concatenate([mixed[:272], rest[16:], rest[:8]], axis=0)
    layer1 = jnp.concatenate([blocks1, mixed[272:], rest[8:16]], axis=0)
    far = swap_core(jnp.where(first, layer1, layer0))
    qkv, qb, vb, proj, inner, ib, outer, rows = assemble(first, jnp.where(first, layer0, layer1), far)

    return (
        edge,
        rows[0][None],
        rows[1][None],
        qkv.T[None],
        qb,
        vb,
        proj[None],
        rows[2][None],
        rows[3][None],
        rows[4][None],
        rows[5][None],
        inner[None],
        ib,
        outer[None],
        rows[6][None],
        rows[7][None],
    )


def solution(mesh):
    grid = Mesh(mesh.devices.reshape(2, 4, 4, 4), ("section", "row", "x", "z"))
    col = ("x", "z")
    by_row = P("section", "row")
    by_col = P("section", col)
    matrix = P("section", "row", col)
    matrix_t = P("section", col, "row")
    return jax.shard_map(
        local,
        mesh=grid,
        in_specs=(
            P(None, col, "row"),
            P(None, col, "row"),
            P(),
            by_row,
            by_row,
            matrix,
            by_col,
            by_col,
            matrix_t,
            by_row,
            by_row,
            by_row,
            by_row,
            matrix,
            by_col,
            matrix_t,
            by_row,
            by_row,
        ),
        out_specs=(
            P("section", None, col, "row"),
            by_row,
            by_row,
            matrix,
            by_col,
            by_col,
            matrix_t,
            by_row,
            by_row,
            by_row,
            by_row,
            matrix,
            by_col,
            matrix_t,
            by_row,
            by_row,
        ),
        check_vma=False,
    )
```
